256 devices in a mesh: gx: 32 (over y, x, core), gy: 8 (over z).
Axes of the slice: x: 4, y: 4, z: 8, core: 2. Of those that a mesh axis runs over, the one named last changes fastest.
Arguments:
- blocks: float32 [32, 8, 8, 128, 128], P('gx', 'gy')
- face_maps: float32 [6, 128, 64], replicated, may hold values from -0.18 to 0.18
- couple: float32 [32, 8, 8, 128, 128], P('gx', 'gy'), may hold values from -0.5 to 0.5
- order_one: int32 [32, 8, 8, 128], P('gx', 'gy'), may hold values from 0 to 127, each once within a row
- count_one: int32 [32, 8, 8], P('gx', 'gy'), may hold values from 16 to 64, as said below
- merge_map: int32 [32, 8, 8], P('gx', 'gy'), may hold values from 0 to 7, as said below
- order_two: int32 [32, 8, 4, 128], P('gx', 'gy'), may hold values from 0 to 127, each once within a row
- count_two: int32 [32, 8, 4], P('gx', 'gy'), may hold values from 16 to 64, as said below
Outputs:
- skeleton_one: float32 [32, 8, 8, 64, 64], P('gx', 'gy')
- skeleton_two: float32 [32, 8, 4, 64, 64], P('gx', 'gy')
The draws below stay inside these ranges and needn't reach their ends.
Inputs may be any that keep to these rules, and one draw needn't show every extreme that they name: Each row of order_one is a permutation of 0 to 127. Each row of order_two is a permutation of 0 to 127. `count_one`: counts are larger on average in the upper half of the first dimension. `count_two`: counts are larger on average in the upper half of the first dimension. For each pair of first-dimension positions 2p and 2p+1 and each y, merge_map at 2p is a permutation of the slots and merge_map at 2p+1 is its inverse.
All inputs are finite; a program needn't handle non-finite values.
Results may differ from the reference program's by a relative error of at most 0.0003.
Values sent between devices are 32-bit elements; how exact they have to be, the bound alone decides.
A program may use at most 64 MiB of HBM per device.

```python
import jax
import jax.numpy as jnp
from jax import lax

M = 128
K = 64
KMIN = 16
BOXES = 8
NBX = 32
NBY = 8


def draw_blocks(key, part):
    first, second = jax.random.split(key)
    shape = (NBX, NBY, BOXES, M, M)
    off = jax.random.uniform(first, shape, jnp.float32, -1.5, 1.5)
    diag = 11.0 + 5.0 * jax.random.uniform(second, shape[:-1], jnp.float32)
    eye = jnp.eye(M, dtype=jnp.float32)
    return off * (1.0 - eye) + eye * diag[..., None]


def skewed_counts(key, slots):
    first, second = jax.random.split(key)
    shape = (NBX, NBY, slots)
    base = jax.random.randint(first, shape, KMIN, K + 1)
    other = jax.random.randint(second, shape, KMIN, K + 1)
    upper = (jnp.arange(NBX, dtype=jnp.int32) >= NBX // 2)[:, None, None]
    counts = jnp.where(upper, jnp.maximum(base, other), base)
    return counts.at[0, 0, 0].set(K).at[0, 0, 1].set(KMIN).astype(jnp.int32)


def draw_count_one(key, part):
    return skewed_counts(jax.random.fold_in(key, 11), BOXES)


def draw_count_two(key, part):
    return skewed_counts(jax.random.fold_in(key, 23), BOXES // 2)


def draw_merge_map(key, part):
    scores = jax.random.randint(jax.random.fold_in(key, 37), (NBX // 2, NBY, BOXES), 0, 1 << 20)
    scores = scores * BOXES + jnp.arange(BOXES, dtype=jnp.int32)
    forward = jnp.argsort(scores, axis=-1).astype(jnp.int32)
    inverse = jnp.argsort(forward, axis=-1).astype(jnp.int32)
    return jnp.stack([forward, inverse], axis=1).reshape(NBX, NBY, BOXES)


def levels(own_key, dims, shards, smallest, top_value):
    factor_of = 1.0
    for position, parts in shards:
        heights = jax.random.uniform(jax.random.fold_in(jax.random.fold_in(own_key, 6), position), (parts,), jnp.float32, smallest / len(shards), top_value / len(shards))
        factor_of = factor_of * jnp.repeat(jnp.exp(heights), dims[position] // parts).reshape((-1,) + (1,) * (len(dims) - 1 - position))
    return factor_of


def normal_values(stream_key, shape, width, limit, cuts=(), held_as=jnp.bfloat16):
    values = jax.random.normal(stream_key, shape, jnp.float32) * width
    if len(cuts) > 0:
        values = levels(stream_key, shape, cuts, -0.22, 0.18) * values
    return jnp.clip(values, min=-limit, max=limit).astype(held_as)


def setup_inputs(seed: int = 0) -> dict:
    streams_of = jax.random.split(jax.random.key(seed), 9)
    blocks = draw_blocks(jax.random.fold_in(streams_of[8], 71), 0)
    face_maps = normal_values(streams_of[1], (6, M, K), 0.03, 0.18, (), jnp.float32)
    couple = normal_values(streams_of[2], (NBX, NBY, BOXES, M, M), M ** -0.5, 0.5, ((0, 32), (1, 8)), jnp.float32)
    order_one = jax.vmap(lambda own: jax.random.permutation(own, M))(jax.random.split(streams_of[3], NBX * NBY * BOXES)).reshape((NBX, NBY, BOXES, M)).astype(jnp.int32)
    count_one = draw_count_one(jax.random.fold_in(streams_of[8], 71), 0)
    merge_map = draw_merge_map(jax.random.fold_in(streams_of[8], 71), 0)
    order_two = jax.vmap(lambda own: jax.random.permutation(own, M))(jax.random.split(streams_of[6], NBX * NBY * (BOXES // 2))).reshape((NBX, NBY, BOXES // 2, M)).astype(jnp.int32)
    count_two = draw_count_two(jax.random.fold_in(streams_of[8], 71), 0)
    return dict(blocks=blocks, face_maps=face_maps, couple=couple, order_one=order_one, count_one=count_one, merge_map=merge_map, order_two=order_two, count_two=count_two)


hp = lax.Precision.HIGHEST


def mat_product(left, right):
    return jnp.einsum('...ij,...jk->...ik', left, right, precision=hp)


def small_inverse(matrix):
    extent = matrix.shape[-1]
    positions = jnp.arange(extent, dtype=jnp.int32)
    reduced = matrix
    inverse = jnp.broadcast_to(jnp.eye(extent, dtype=matrix.dtype), matrix.shape)
    for step in range(extent):
        pivot = reduced[..., step, step]
        pivot_row = reduced[..., step, :] / pivot[..., None]
        pivot_inv = inverse[..., step, :] / pivot[..., None]
        factor = jnp.where(positions == step, 0.0, reduced[..., :, step])
        reduced = reduced - factor[..., :, None] * pivot_row[..., None, :]
        inverse = inverse - factor[..., :, None] * pivot_inv[..., None, :]
        chosen = (positions == step)[:, None]
        reduced = jnp.where(chosen, pivot_row[..., None, :], reduced)
        inverse = jnp.where(chosen, pivot_inv[..., None, :], inverse)
    return inverse


def spd_inverse(matrix):
    extent = matrix.shape[-1]
    if extent <= 8:
        return small_inverse(matrix)
    middle = extent // 2
    upper = matrix[..., :middle, :middle]
    corner = matrix[..., :middle, middle:]
    lower = matrix[..., middle:, middle:]
    first_inv = spd_inverse(upper)
    solved = mat_product(first_inv, corner)
    schur = lower - mat_product(jnp.swapaxes(corner, -1, -2), solved)
    schur_inv = spd_inverse(schur)
    top_right = -mat_product(solved, schur_inv)
    top_left = first_inv - mat_product(top_right, jnp.swapaxes(solved, -1, -2))
    top = jnp.concatenate([top_left, top_right], axis=-1)
    bottom = jnp.concatenate([jnp.swapaxes(top_right, -1, -2), schur_inv], axis=-1)
    return jnp.concatenate([top, bottom], axis=-2)


def select_maps(order, count):
    cols = jnp.arange(M, dtype=jnp.int32)
    hit = order[..., None, :] == cols[:, None]
    live = (cols < count[..., None])[..., None, :]
    skel = jnp.where(hit & live, 1.0, 0.0).astype(jnp.float32)[..., :K]
    rest = jnp.where(hit & (~live), 1.0, 0.0).astype(jnp.float32)
    pad = jnp.where(jnp.arange(K, dtype=jnp.int32) >= count[..., None], 1.0, 0.0).astype(jnp.float32)
    return skel, rest, pad


def skeleton_block(block, order, count):
    skel, rest, pad = select_maps(order, count)
    inner = jnp.einsum('...ij,...jk->...ik', block, skel, precision=hp)
    return jnp.einsum('...ji,...jk->...ik', skel, inner, precision=hp)


def skeletonize(block, order, count):
    skel, rest, pad = select_maps(order, count)
    a_skel = jnp.einsum('...ij,...jk->...ik', block, skel, precision=hp)
    a_rest = jnp.einsum('...ij,...jk->...ik', block, rest, precision=hp)
    eye = jnp.eye(K, dtype=jnp.float32)
    normal = jnp.einsum('...ji,...jk->...ik', a_skel, a_skel, precision=hp) + pad[..., :, None] * eye
    rhs = jnp.einsum('...ji,...jk->...ik', a_skel, a_rest, precision=hp)
    interp = mat_product(spd_inverse(normal), rhs)
    weights = skel + jnp.einsum('...ij,...kj->...ik', rest, interp, precision=hp)
    applied = jnp.einsum('...ij,...jk->...ik', block, weights, precision=hp)
    result = jnp.einsum('...ji,...jk->...ik', weights, applied, precision=hp) + pad[..., :, None] * eye
    return result, weights


def face_term(face, near):
    left = jnp.einsum('ik,...kl->...il', face, near, precision=hp)
    return jnp.einsum('...il,jl->...ij', left, face, precision=hp)


def reference(blocks, face_maps, couple, order_one, count_one, merge_map, order_two, count_two):
    s_all = lax.map(lambda x: skeleton_block(blocks[x], order_one[x], count_one[x]), jnp.arange(NBX))
    s_pad = jnp.pad(s_all, ((1, 1), (1, 1), (1, 1), (0, 0), (0, 0)))

    def level_one(x):
        row = lax.dynamic_slice_in_dim(s_pad, x, 3, 0)
        near = [row[0, 1:-1, 1:-1], row[2, 1:-1, 1:-1], row[1, :-2, 1:-1], row[1, 2:, 1:-1], row[1, 1:-1, :-2], row[1, 1:-1, 2:]]
        updated = blocks[x]
        for face in range(6):
            updated = updated - face_term(face_maps[face], near[face])
        result, weights = skeletonize(updated, order_one[x], count_one[x])
        across = jnp.einsum('...ji,...jk->...ik', weights, couple[x], precision=hp)
        return result, weights, across

    skeleton_one, weights, across = lax.map(level_one, jnp.arange(NBX))
    mapping = merge_map[0::2]

    def partner(field):
        return jnp.take_along_axis(field[1::2], mapping[..., None, None], axis=2)

    z_a, w_a, v_a = skeleton_one[0::2], weights[0::2], across[0::2]
    z_b, w_b, v_b = partner(skeleton_one), partner(weights), partner(across)
    cross = jnp.einsum('...km,...ml->...kl', v_a, w_b, precision=hp)
    cross = cross + jnp.einsum('...lm,...mk->...kl', v_b, w_a, precision=hp)
    top = jnp.concatenate([z_a, cross], axis=-1)
    bottom = jnp.concatenate([jnp.swapaxes(cross, -1, -2), z_b], axis=-1)
    parents = jnp.concatenate([top, bottom], axis=-2)
    parents = parents.reshape(NBX // 2, NBY, 2, BOXES // 2, M, M).transpose(0, 2, 1, 3, 4, 5).reshape(NBX, NBY, BOXES // 2, M, M)
    skeleton_two = lax.map(lambda x: skeletonize(parents[x], order_two[x], count_two[x])[0], jnp.arange(NBX))
    return skeleton_one, skeleton_two
```

```python
import functools

import jax
import jax.numpy as jnp
from jax import lax
from jax.experimental import pallas as pl
from jax.experimental.pallas import tpu as pltpu
from jax.sharding import PartitionSpec as P

MESH = pl.DeviceIdType.MESH
BF = jnp.bfloat16
F32 = jnp.float32
NN = (((1,), (0,)), ((), ()))
NT = (((1,), (1,)), ((), ()))
K = 64
M = 128


def dot(left, right, dims):
    return lax.dot_general(left, right, dims, preferred_element_type=F32)


def split(x):
    high = x.astype(BF)
    low = (x - high.astype(F32)).astype(BF)
    return high, low


def lanes(*parts):
    return jnp.concatenate(parts, axis=1)


def rows(*parts):
    return jnp.concatenate(parts, axis=0)


def nn3(left, right):
    lh, ll = left
    rh, rl = right
    return dot(lanes(lh, ll, lh), rows(rh, rh, rl), NN)


def nt3(left, right):
    lh, ll = left
    rh, rl = right
    return dot(lanes(lh, ll, lh), lanes(rh, rh, rl), NT)


def iota(shape, dim):
    return lax.broadcasted_iota(jnp.int32, shape, dim)


def invert(pairs):
    count = len(pairs)
    left = iota((1, M), 1) < K
    scales = []
    tiles = [[] for _ in range(8)]
    for n in pairs:
        top = jnp.max(n, axis=0, keepdims=True)
        first = jnp.max(jnp.where(left, top, 0.0), axis=1, keepdims=True)
        second = jnp.max(jnp.where(left, 0.0, top), axis=1, keepdims=True)
        scale = 1.0 / jnp.where(left, first, second)
        scales.append(scale)
        n = n * scale
        for i in range(8):
            tiles[i].append(n[8 * i : 8 * i + 8])
    tiles = [jnp.stack(t) for t in tiles]
    lane = iota((count, 8, M), 2)
    half = jnp.where(lane >= K, K, 0)
    within = iota((count, 1, M), 2) % K
    sub = iota((count, 8, M), 1)

    def body(t, tiles):
        tiles = list(tiles)
        for q in range(8):
            step = t * 8 + q
            place = half + step
            cols = [jnp.take_along_axis(x, place, axis=2, mode="promise_in_bounds") for x in tiles]
            row = tiles[0][:, q : q + 1, :]
            inverse = 1.0 / cols[0][:, q : q + 1, :]
            row = jnp.where(within == step, 1.0 + inverse, row * inverse)
            cols[0] = jnp.where(sub == q, cols[0] - 1.0, cols[0])
            tiles = [x - c * row for x, c in zip(tiles, cols)]
        return tuple(tiles[1:] + tiles[:1])

    tiles = lax.fori_loop(0, 8, body, tuple(tiles))
    return [
        rows(*[tiles[i][p] for i in range(8)]) * scales[p] for p in range(count)
    ]


def skeletonize(read_block, turn_of, counts, write):
    boxes = len(counts)
    row_of = iota((K, M), 0)
    lane_of = iota((K, M), 1)
    left = lane_of < K
    diagonal = (lane_of % K) == row_of
    normals, sides = [], []
    for b in range(0, boxes, 2):
        halves = []
        for i in (0, 1):
            c = counts[b + i]
            ah, al = split(read_block(b + i))
            turn = turn_of(b + i)
            turned = split(dot(lanes(turn, turn), lanes(ah, al), NT))
            skel = tuple(jnp.where(row_of < c, x[:K], jnp.zeros_like(x[:K])) for x in turned)
            gram = nt3(skel, turned)
            sides.append(jnp.where(lane_of >= c, gram, 0.0))
            normal = jnp.where(lane_of < c, gram, 0.0)
            if i == 1:
                normal = pltpu.roll(normal, K, 1)
                c_here = counts[b + 1]
            halves.append(normal)
        padded = jnp.where(row_of >= jnp.where(left, counts[b], counts[b + 1]), 1.0, 0.0)
        normals.append(
            jnp.where(left, halves[0], halves[1]) + jnp.where(diagonal, padded, 0.0)
        )
    inverses = invert(normals)
    for b in range(0, boxes, 2):
        zero = jnp.zeros((K, M), BF)
        firsts, seconds = split(sides[b]), split(sides[b + 1])
        right = tuple(
            rows(lanes(f, zero), lanes(zero, s)) for f, s in zip(firsts, seconds)
        )
        interp = nn3(split(inverses[b // 2]), right)
        for i in (0, 1):
            c = counts[b + i]
            keep = jnp.where((lane_of == row_of) & (row_of < c), 1.0, 0.0)
            short = split(interp[:, M * i : M * i + M] + keep)
            turn = turn_of(b + i)
            weights = dot(lanes(*short), rows(turn, turn), NN)
            parts = split(weights)
            applied = split(nn3(parts, split(read_block(b + i))))
            twice = tuple(rows(x, x) for x in parts)
            pad = jnp.where(diagonal & (row_of >= c), 1.0, 0.0)
            write(b + i, nt3(applied, twice) + pad, weights)


def kernel(
    sizes,
    blocks_hbm, faces_hbm, couple_hbm, order_one, count_one, merge_map, order_two, count_two,
    out_one, out_two,
    a_ref, face_ref, c_ref, turn_ref, own_ref, near_ref, send_c, near_c, mixed_ref,
    q_ref, child_ref, send_child, level_ref, parent_ref,
    load_sems, send_sems, recv_sems,
):
    nx, ny = sizes
    gx, gy = lax.axis_index("gx"), lax.axis_index("gy")
    odd = gx % 2
    boxes = 8
    parents = 4

    loads = [pltpu.make_async_copy(blocks_hbm.at[0, 0, b], a_ref.at[b], load_sems.at[b]) for b in range(boxes)]
    load_face = pltpu.make_async_copy(faces_hbm, face_ref, load_sems.at[8])
    load_c = pltpu.make_async_copy(couple_hbm.at[0, 0], c_ref, load_sems.at[9])
    for load in loads:
        load.start()
    load_face.start()
    load_c.start()

    barrier = pltpu.get_barrier_semaphore()
    sides = (
        (gx > 0, {"gx": gx - 1, "gy": gy}, 1),
        (gx < nx - 1, {"gx": gx + 1, "gy": gy}, 0),
        (gy > 0, {"gx": gx, "gy": gy - 1}, 3),
        (gy < ny - 1, {"gx": gx, "gy": gy + 1}, 2),
    )
    partner = {"gx": gx + 1 - 2 * odd, "gy": gy}
    for there, where, _ in sides:
        @pl.when(there)
        def _(where=where):
            pl.semaphore_signal(barrier, inc=1, device_id=where, device_id_type=MESH)

    orders = rows(
        order_one[0, 0].astype(F32), order_two[0, 0].astype(F32), jnp.zeros((4, M), F32)
    ).T
    lane = iota((M, M), 1).astype(F32)
    for b in range(boxes + parents):
        turn_ref[b] = jnp.where(orders[:, b : b + 1] == lane, 1.0, 0.0).astype(BF)

    row_of = iota((K, M), 0)
    lane_of = iota((K, M), 1)
    left = lane_of < K
    counts = [count_one[0, 0, b] for b in range(boxes)]

    def copies(part):
        got = []
        for d, (there, where, face) in enumerate(sides):
            got.append((there, pltpu.make_async_remote_copy(
                src_ref=own_ref.at[part],
                dst_ref=near_ref.at[face, part],
                send_sem=send_sems.at[2 * d + part],
                recv_sem=recv_sems.at[2 * face + part],
                device_id=where,
                device_id_type=MESH,
            )))
        return got

    for part in range(2):
        for b in range(4 * part, 4 * part + 4, 2):
            halves = []
            for i in (0, 1):
                loads[b + i].wait()
                turn = turn_ref[b + i]
                ah, al = split(a_ref[b + i])
                picked = split(dot(lanes(turn[:K], turn[:K]), rows(ah, al), NN))
                other = turn if i == 0 else rows(turn[K:], turn[:K])
                halves.append(dot(lanes(*picked), lanes(other, other), NT))
            c = jnp.where(left, counts[b], counts[b + 1])
            s = jnp.where(left, halves[0], halves[1])
            s = jnp.where((row_of < c) & (lane_of % K < c), s, 0.0)
            own_ref[part, (b % 4) // 2 * K : (b % 4) // 2 * K + K, :] = s
        if part == 0:
            pl.semaphore_wait(
                barrier,
                (gx + nx - 1) // nx + (2 * nx - 2 - gx) // nx
                + (gy + ny - 1) // ny + (2 * ny - 2 - gy) // ny,
            )
        for there, copy in reversed(copies(part)):
            @pl.when(there)
            def _(copy=copy):
                copy.start()

    m = [merge_map[0, 0, b] for b in range(boxes)]
    found = []
    for k in range(boxes):
        at = jnp.int32(0)
        for b in range(1, boxes):
            at = jnp.where(m[b] == k, b, at)
        found.append(at)
    is_odd = odd == 1
    send_box = [jnp.where(is_odd, found[k], k + 4) for k in range(parents)]
    keep_box = [jnp.where(is_odd, found[k + 4], k) for k in range(parents)]

    load_c.wait()
    for k in range(parents):
        send_c[k] = c_ref[send_box[k]]
    couple_copy = pltpu.make_async_remote_copy(
        src_ref=send_c, dst_ref=near_c, send_sem=send_sems.at[8], recv_sem=recv_sems.at[8],
        device_id=partner, device_id_type=MESH,
    )
    couple_copy.start()

    for there, _, face in sides:
        @pl.when(jnp.logical_not(there))
        def _(face=face):
            near_ref[face ^ 1] = jnp.zeros((2, 2 * K, M), F32)

    load_face.wait()

    def project(f, source):
        face = split(face_ref[f])
        zero = jnp.zeros((M, K), BF)
        right = tuple(rows(lanes(x, zero), lanes(zero, x)) for x in face)
        return nt3(split(source), right)

    for f in (4, 5):
        q = project(f, own_ref[...].reshape(4 * K, M))
        for b in range(boxes):
            p, i = b // 2, b % 2
            n = b + 1 if f == 4 else b - 1
            if 0 <= n < boxes:
                q_ref[n // 2, f * K : f * K + K, M * (n % 2) : M * (n % 2) + M] = (
                    q[p * K : p * K + K, M * i : M * i + M]
                )
        edge = 0 if f == 4 else boxes - 1
        q_ref[edge // 2, f * K : f * K + K, M * (edge % 2) : M * (edge % 2) + M] = jnp.zeros((K, M), F32)

    for f in range(4):
        there = sides[f][0]
        for part in range(2):
            @pl.when(there)
            def _(f=f, part=part):
                pltpu.make_async_remote_copy(
                    src_ref=own_ref.at[part],
                    dst_ref=near_ref.at[f, part],
                    send_sem=send_sems.at[2 * f + part],
                    recv_sem=recv_sems.at[2 * f + part],
                    device_id=sides[f][1],
                    device_id_type=MESH,
                ).wait_recv()
        q = project(f, near_ref[f].reshape(4 * K, M))
        for p in range(4):
            q_ref[p, f * K : f * K + K, :] = q[p * K : p * K + K]

    all_faces = split(lanes(*[face_ref[f] for f in range(6)]))
    for p in range(4):
        d = nn3(all_faces, split(q_ref[p]))
        for i in (0, 1):
            a_ref[2 * p + i] = a_ref[2 * p + i] - d[:, M * i : M * i + M]

    def write_one(b, z, w):
        level_ref[b, :K] = z
        level_ref[b, K:] = w
        out_one[0, 0, b] = z[:, :K]

    skeletonize(lambda b: a_ref[b], lambda b: turn_ref[b], counts, write_one)

    for k in range(parents):
        send_child[k] = level_ref[send_box[k]]
    child_copy = pltpu.make_async_remote_copy(
        src_ref=send_child, dst_ref=child_ref.at[odd], send_sem=send_sems.at[9],
        recv_sem=recv_sems.at[9], device_id=partner, device_id_type=MESH,
    )
    child_copy.start()

    couple_copy.wait_recv()
    for k in range(parents):
        mine, other = c_ref[keep_box[k]], near_c[k]
        first = jnp.where(is_odd, other, mine)
        second = jnp.where(is_odd, mine, other)
        mixed_ref[k] = first + second.T
        child_ref[odd, k] = level_ref[keep_box[k]]

    child_copy.wait_recv()
    for k in range(parents):
        w_a = split(child_ref[0, k, K:])
        w_b = split(child_ref[1, k, K:])
        h = split(nn3(w_a, split(mixed_ref[k])))
        cross = nt3(h, tuple(rows(x, x) for x in w_b))
        turned = nt3(w_b, tuple(rows(x, x) for x in h))
        parent_ref[k, :K] = jnp.where(left, child_ref[0, k, :K], cross)
        parent_ref[k, K:] = jnp.where(left, turned, child_ref[1, k, :K])

    def write_two(k, z, w):
        out_two[0, 0, k] = z[:, :K]

    skeletonize(
        lambda k: parent_ref[k], lambda k: turn_ref[boxes + k],
        [count_two[0, 0, k] for k in range(parents)], write_two,
    )

    for part in range(2):
        for there, copy in copies(part):
            @pl.when(there)
            def _(copy=copy):
                copy.wait_send()
    couple_copy.wait_send()
    child_copy.wait_send()


def shards(sizes, *args):
    vmem = pl.BlockSpec(memory_space=pltpu.VMEM)
    smem = pl.BlockSpec(memory_space=pltpu.SMEM)
    anyw = pl.BlockSpec(memory_space=pl.ANY)
    return pl.pallas_call(
        functools.partial(kernel, sizes),
        out_shape=(
            jax.ShapeDtypeStruct((1, 1, 8, K, K), F32),
            jax.ShapeDtypeStruct((1, 1, 4, K, K), F32),
        ),
        in_specs=[anyw, anyw, anyw, vmem, smem, smem, vmem, smem],
        out_specs=(vmem, vmem),
        scratch_shapes=[
            pltpu.VMEM((8, M, M), F32),
            pltpu.VMEM((6, M, K), F32),
            pltpu.VMEM((8, M, M), F32),
            pltpu.VMEM((12, M, M), BF),
            pltpu.VMEM((2, 2 * K, M), F32),
            pltpu.VMEM((4, 2, 2 * K, M), F32),
            pltpu.VMEM((4, M, M), F32),
            pltpu.VMEM((4, M, M), F32),
            pltpu.VMEM((4, M, M), F32),
            pltpu.VMEM((4, 6 * K, 2 * M), F32),
            pltpu.VMEM((2, 4, M, M), F32),
            pltpu.VMEM((4, M, M), F32),
            pltpu.VMEM((8, M, M), F32),
            pltpu.VMEM((4, M, M), F32),
            pltpu.SemaphoreType.DMA((10,)),
            pltpu.SemaphoreType.DMA((10,)),
            pltpu.SemaphoreType.DMA((10,)),
        ],
        compiler_params=pltpu.CompilerParams(
            collective_id=0, has_side_effects=True, vmem_limit_bytes=32 << 20
        ),
        name="factor",
    )(*args)


def solution(mesh):
    return jax.shard_map(
        functools.partial(shards, (mesh.shape["gx"], mesh.shape["gy"])),
        mesh=mesh,
        in_specs=(
            P("gx", "gy", None, None, None),
            P(),
            P("gx", "gy", None, None, None),
            P("gx", "gy", None, None),
            P("gx", "gy", None),
            P("gx", "gy", None),
            P("gx", "gy", None, None),
            P("gx", "gy", None),
        ),
        out_specs=(P("gx", "gy", None, None, None), P("gx", "gy", None, None, None)),
        check_vma=False,
    )
```

```python
import functools

import jax
import jax.numpy as jnp
from jax import lax
from jax.experimental import pallas as pl
from jax.experimental.pallas import tpu as pltpu
from jax.sharding import PartitionSpec as P

MESH = pl.DeviceIdType.MESH
BF = jnp.bfloat16
F32 = jnp.float32
NN = (((1,), (0,)), ((), ()))
NT = (((1,), (1,)), ((), ()))
K = 64
M = 128
W = 32


def dot(left, right, dims):
    return lax.dot_general(left, right, dims, preferred_element_type=F32)


def split(x):
    high = x.astype(BF)
    low = (x - high.astype(F32)).astype(BF)
    return high, low


def lanes(*parts):
    return jnp.concatenate(parts, axis=1)


def rows(*parts):
    return jnp.concatenate(parts, axis=0)


def nn3(left, right):
    lh, ll = left
    rh, rl = right
    return dot(lanes(lh, ll, lh), rows(rh, rh, rl), NN)


def nt3(left, right):
    lh, ll = left
    rh, rl = right
    return dot(lanes(lh, ll, lh), lanes(rh, rh, rl), NT)


def iota(shape, dim):
    return lax.broadcasted_iota(jnp.int32, shape, dim)


def shifted(x, amount):
    amount = amount % M
    if amount == 0:
        return x
    return rows(x[M - amount :], x[: M - amount])


def invert(groups):
    n = len(groups)
    lane = iota((1, M), 1)
    scales = []
    for group in groups:
        top = jnp.maximum(*[jnp.max(x, axis=0, keepdims=True) for x in group])
        scale = jnp.ones((1, M), F32)
        for s in range(M // W):
            inside = lane // W == s
            scale = jnp.where(
                inside, jnp.max(jnp.where(inside, top, 0.0), axis=1, keepdims=True), scale
            )
        scales.append(1.0 / scale)
    tiles = [
        [jnp.stack([g[j][8 * i : 8 * i + 8] * sc for g, sc in zip(groups, scales)]) for j in range(2)]
        for i in range(8)
    ]
    sub = iota((n, 8, M), 1)
    within = iota((n, 8, M), 2) % W
    segment = iota((8 * n, 8, M), 2) // W * W
    for t in range(8):
        here, first = divmod(8 * t, W)
        source = jnp.concatenate([tiles[i][here] for i in range(8)], axis=0)
        cols = []
        for q in range(8):
            got = jnp.take_along_axis(source, segment + (first + q), axis=2, mode="promise_in_bounds")
            cols.append([got[n * i : n * i + n] for i in range(8)])
        unit = within == sub + first
        x = list(tiles[t])
        x[here] = jnp.where(
            (within >= first) & (within < first + 8), jnp.where(unit, 1.0, 0.0), x[here]
        )
        c = [cols[q][t] for q in range(8)]
        for k in range(8):
            inverse = 1.0 / c[k][:, k : k + 1, :]
            factor = jnp.where(sub == k, c[k] - 1.0, c[k])
            for q in range(k + 1, 8):
                c[q] = c[q] - factor * (c[q][:, k : k + 1, :] * inverse)
            x = [v - factor * (v[:, k : k + 1, :] * inverse) for v in x]
        r = list(x)
        r[here] = jnp.where(unit, x[here] + 1.0, x[here])
        for i in [(t + 1 + step) % 8 for step in range(7)]:
            for j in range(2):
                terms = [cols[q][i] * r[j][:, q : q + 1, :] for q in range(8)]
                while len(terms) > 1:
                    terms = [one + two for one, two in zip(terms[::2], terms[1::2])]
                tiles[i][j] = tiles[i][j] - terms[0]
        tiles[t] = x
    return [
        [jnp.concatenate([tiles[i][j][p] for i in range(8)], axis=0) * scales[p] for j in range(2)]
        for p in range(n)
    ]


def skeletonize(read_block, turn_of, counts, write):
    boxes = len(counts)
    row_of = iota((K, M), 0)
    lane_of = iota((K, M), 1)
    inner = lane_of % W
    segment = lane_of // W
    natural = [(lane_of + (M - W * r)) % M for r in range(4)]
    groups, sides = [], []
    for g in range(0, boxes, 4):
        grams = []
        for r in range(4):
            ah, al = split(read_block(g + r))
            turn = turn_of(g + r)
            turned = split(dot(lanes(turn, turn), lanes(ah, al), NT))
            skel = tuple(
                jnp.where(row_of < counts[g + r], y, jnp.zeros_like(y))
                for y in (shifted(x, -W * r)[:K] for x in turned)
            )
            gram = nt3(skel, tuple(rows(x, shifted(x, -W)) for x in turned))
            sides.append(jnp.where(natural[r] >= counts[g + r], gram[:, :M], 0.0))
            grams.append(gram)
        count = jnp.where(
            segment < 2,
            jnp.where(segment == 0, counts[g], counts[g + 1]),
            jnp.where(segment == 2, counts[g + 2], counts[g + 3]),
        )
        group = []
        for j in range(2):
            parts = [x[:, M * j : M * j + M] for x in grams]
            normal = jnp.where(
                segment < 2,
                jnp.where(segment == 0, parts[0], parts[1]),
                jnp.where(segment == 2, parts[2], parts[3]),
            )
            column = inner + W * j
            normal = jnp.where(column < count, normal, 0.0)
            group.append(normal + jnp.where((column == row_of) & (row_of >= count), 1.0, 0.0))
        groups.append(group)
    inverses = invert(groups)
    for g in range(0, boxes, 4):
        inverse = split(lanes(*inverses[g // 4]))
        seg = iota((K, 2 * M), 1) % M // W
        stacked = tuple(
            rows(*[jnp.where(seg == r, x, jnp.zeros_like(x)) for r in range(4)]) for x in inverse
        )
        right = [split(sides[g + r]) for r in range(4)]
        right = tuple(
            rows(*[right[r][h][W * j : W * j + W] for j in range(2) for r in range(4)])
            for h in range(2)
        )
        interp = nn3(stacked, right)
        for r in range(4):
            b = g + r
            c = counts[b]
            keep = jnp.where((natural[r] == row_of) & (row_of < c), 1.0, 0.0)
            short = split(interp[K * r : K * r + K] + keep)
            turn = turn_of(b)
            weights = dot(lanes(*short), rows(turn, turn), NN)
            parts = split(weights)
            applied = split(nn3(parts, split(read_block(b))))
            twice = tuple(rows(x, x) for x in parts)
            pad = jnp.where((lane_of % K == row_of) & (row_of >= c), 1.0, 0.0)
            write(b, nt3(applied, twice) + pad, weights)


def kernel(
    sizes,
    blocks_hbm, faces_hbm, couple_hbm, small_a, small_b, small_c, small_d, small_e,
    out_one, out_two,
    a_ref, face_ref, c_ref, turn_ref, own_ref, near_ref, send_c, near_c, mixed_ref,
    q_ref, child_ref, send_child, level_ref, parent_ref,
    order_one, order_two, count_one, count_two, merge_map,
    load_sems, send_sems, recv_sems,
):
    nx, ny = sizes
    gx, gy = lax.axis_index("gx"), lax.axis_index("gy")
    odd = gx % 2
    boxes = 8
    parents = 4

    loads = [pltpu.make_async_copy(blocks_hbm.at[0, 0, b], a_ref.at[b], load_sems.at[b]) for b in range(boxes)]
    load_face = pltpu.make_async_copy(faces_hbm, face_ref, load_sems.at[8])
    load_c = pltpu.make_async_copy(couple_hbm.at[0, 0], c_ref, load_sems.at[9])
    small_loads = [
        pltpu.make_async_copy(source, target, load_sems.at[10 + i])
        for i, (source, target) in enumerate(
            zip(
                (small_a, small_b, small_c, small_d, small_e),
                (order_one, count_one, merge_map, order_two, count_two),
            )
        )
    ]
    for load in small_loads + loads:
        load.start()
    load_face.start()
    load_c.start()

    barrier = pltpu.get_barrier_semaphore()
    sides = (
        (gx > 0, {"gx": gx - 1, "gy": gy}, 1),
        (gx < nx - 1, {"gx": gx + 1, "gy": gy}, 0),
        (gy > 0, {"gx": gx, "gy": gy - 1}, 3),
        (gy < ny - 1, {"gx": gx, "gy": gy + 1}, 2),
    )
    partner = {"gx": gx + 1 - 2 * odd, "gy": gy}
    for there, where, _ in sides:
        @pl.when(there)
        def _(where=where):
            pl.semaphore_signal(barrier, inc=1, device_id=where, device_id_type=MESH)

    for load in small_loads:
        load.wait()
    orders = rows(
        order_one[0, 0].astype(F32), order_two[0, 0].astype(F32), jnp.zeros((4, M), F32)
    ).T
    lane = iota((M, M), 1).astype(F32)
    for b in range(boxes + parents):
        turn_ref[b] = shifted(jnp.where(orders[:, b : b + 1] == lane, 1.0, 0.0).astype(BF), W * (b % 4))

    row_of = iota((K, M), 0)
    lane_of = iota((K, M), 1)
    left = lane_of < K
    counts = [count_one[0, 0, b] for b in range(boxes)]

    def copies(part):
        got = []
        for d, (there, where, face) in enumerate(sides):
            got.append((there, pltpu.make_async_remote_copy(
                src_ref=own_ref.at[part],
                dst_ref=near_ref.at[face, part],
                send_sem=send_sems.at[2 * d + part],
                recv_sem=recv_sems.at[2 * face + part],
                device_id=where,
                device_id_type=MESH,
            )))
        return got

    for part in range(2):
        for b in range(4 * part, 4 * part + 4, 2):
            halves = []
            for i in (0, 1):
                loads[b + i].wait()
                turn = shifted(turn_ref[b + i], -W * ((b + i) % 4))
                ah, al = split(a_ref[b + i])
                picked = split(dot(lanes(turn[:K], turn[:K]), rows(ah, al), NN))
                other = turn if i == 0 else rows(turn[K:], turn[:K])
                halves.append(dot(lanes(*picked), lanes(other, other), NT))
            c = jnp.where(left, counts[b], counts[b + 1])
            s = jnp.where(left, halves[0], halves[1])
            s = jnp.where((row_of < c) & (lane_of % K < c), s, 0.0)
            own_ref[part, (b % 4) // 2 * K : (b % 4) // 2 * K + K, :] = s
        if part == 0:
            pl.semaphore_wait(
                barrier,
                (gx + nx - 1) // nx + (2 * nx - 2 - gx) // nx
                + (gy + ny - 1) // ny + (2 * ny - 2 - gy) // ny,
            )
        for there, copy in reversed(copies(part)):
            @pl.when(there)
            def _(copy=copy):
                copy.start()

    m = [merge_map[0, 0, b] for b in range(boxes)]
    found = []
    for k in range(boxes):
        at = jnp.int32(0)
        for b in range(1, boxes):
            at = jnp.where(m[b] == k, b, at)
        found.append(at)
    is_odd = odd == 1
    send_box = [jnp.where(is_odd, found[k], k + 4) for k in range(parents)]
    keep_box = [jnp.where(is_odd, found[k + 4], k) for k in range(parents)]

    load_c.wait()
    for k in range(parents):
        send_c[k] = c_ref[send_box[k]]
    couple_copy = pltpu.make_async_remote_copy(
        src_ref=send_c, dst_ref=near_c, send_sem=send_sems.at[8], recv_sem=recv_sems.at[8],
        device_id=partner, device_id_type=MESH,
    )
    couple_copy.start()

    for there, _, face in sides:
        @pl.when(jnp.logical_not(there))
        def _(face=face):
            near_ref[face ^ 1] = jnp.zeros((2, 2 * K, M), F32)

    load_face.wait()

    def mix_couples():
        couple_copy.wait_recv()
        for k in range(parents):
            mine, other = c_ref[keep_box[k]], near_c[k]
            first = jnp.where(is_odd, other, mine)
            second = jnp.where(is_odd, mine, other)
            mixed_ref[k] = first + second.T

    def project(f, source):
        face = split(face_ref[f])
        zero = jnp.zeros((K, M), BF)
        right = tuple(rows(lanes(x, zero), lanes(zero, x)) for x in face)
        return nn3(split(source), right)

    all_faces = split(face_ref[...].reshape(6 * K, M).T)
    for f in (4, 5):
        q = project(f, own_ref[...].reshape(4 * K, M))
        for b in range(boxes):
            p, i = b // 2, b % 2
            n = b + 1 if f == 4 else b - 1
            if 0 <= n < boxes:
                q_ref[n // 2, f * K : f * K + K, M * (n % 2) : M * (n % 2) + M] = (
                    q[p * K : p * K + K, M * i : M * i + M]
                )
        edge = 0 if f == 4 else boxes - 1
        q_ref[edge // 2, f * K : f * K + K, M * (edge % 2) : M * (edge % 2) + M] = jnp.zeros((K, M), F32)

    for f in range(4):
        if f == 2:
            mix_couples()
        there = sides[f][0]
        for part in range(2):
            @pl.when(there)
            def _(f=f, part=part):
                pltpu.make_async_remote_copy(
                    src_ref=own_ref.at[part],
                    dst_ref=near_ref.at[f, part],
                    send_sem=send_sems.at[2 * f + part],
                    recv_sem=recv_sems.at[2 * f + part],
                    device_id=sides[f][1],
                    device_id_type=MESH,
                ).wait_recv()
        q = project(f, near_ref[f].reshape(4 * K, M))
        for p in range(4):
            q_ref[p, f * K : f * K + K, :] = q[p * K : p * K + K]

    for p in range(4):
        d = nn3(all_faces, split(q_ref[p]))
        for i in (0, 1):
            a_ref[2 * p + i] = a_ref[2 * p + i] - d[:, M * i : M * i + M]

    def write_one(b, z, w):
        level_ref[b, :K] = z
        level_ref[b, K:] = w
        out_one[0, 0, b] = z[:, :K]

    skeletonize(lambda b: a_ref[b], lambda b: turn_ref[b], counts, write_one)

    for k in range(parents):
        send_child[k] = level_ref[send_box[k]]
    child_copy = pltpu.make_async_remote_copy(
        src_ref=send_child, dst_ref=child_ref.at[odd], send_sem=send_sems.at[9],
        recv_sem=recv_sems.at[9], device_id=partner, device_id_type=MESH,
    )
    child_copy.start()

    for k in range(parents):
        child_ref[odd, k] = level_ref[keep_box[k]]

    child_copy.wait_recv()
    for k in range(parents):
        w_a = split(child_ref[0, k, K:])
        w_b = split(child_ref[1, k, K:])
        h = split(nn3(w_a, split(mixed_ref[k])))
        cross = nt3(h, tuple(rows(x, x) for x in w_b))
        turned = nt3(w_b, tuple(rows(x, x) for x in h))
        parent_ref[k, :K] = jnp.where(left, child_ref[0, k, :K], cross)
        parent_ref[k, K:] = jnp.where(left, turned, child_ref[1, k, :K])

    def write_two(k, z, w):
        out_two[0, 0, k] = z[:, :K]

    skeletonize(
        lambda k: parent_ref[k], lambda k: turn_ref[boxes + k],
        [count_two[0, 0, k] for k in range(parents)], write_two,
    )

    for part in range(2):
        for there, copy in copies(part):
            @pl.when(there)
            def _(copy=copy):
                copy.wait_send()
    couple_copy.wait_send()
    child_copy.wait_send()


def shards(sizes, blocks, face_maps, *others):
    vmem = pl.BlockSpec(memory_space=pltpu.VMEM)
    hbm = pl.BlockSpec(memory_space=pltpu.HBM)
    return pl.pallas_call(
        functools.partial(kernel, sizes),
        out_shape=(
            jax.ShapeDtypeStruct((1, 1, 8, K, K), F32),
            jax.ShapeDtypeStruct((1, 1, 4, K, K), F32),
        ),
        in_specs=[hbm] * 8,
        out_specs=(vmem, vmem),
        scratch_shapes=[
            pltpu.VMEM((8, M, M), F32),
            pltpu.VMEM((6, K, M), F32),
            pltpu.VMEM((8, M, M), F32),
            pltpu.VMEM((12, M, M), BF),
            pltpu.VMEM((2, 2 * K, M), F32),
            pltpu.VMEM((4, 2, 2 * K, M), F32),
            pltpu.VMEM((4, M, M), F32),
            pltpu.VMEM((4, M, M), F32),
            pltpu.VMEM((4, M, M), F32),
            pltpu.VMEM((4, 6 * K, 2 * M), F32),
            pltpu.VMEM((2, 4, M, M), F32),
            pltpu.VMEM((4, M, M), F32),
            pltpu.VMEM((8, M, M), F32),
            pltpu.VMEM((4, M, M), F32),
            pltpu.VMEM((1, 1, 8, M), jnp.int32),
            pltpu.VMEM((1, 1, 4, M), jnp.int32),
            pltpu.SMEM((1, 1, 8), jnp.int32),
            pltpu.SMEM((1, 1, 4), jnp.int32),
            pltpu.SMEM((1, 1, 8), jnp.int32),
            pltpu.SemaphoreType.DMA((15,)),
            pltpu.SemaphoreType.DMA((10,)),
            pltpu.SemaphoreType.DMA((10,)),
        ],
        compiler_params=pltpu.CompilerParams(
            collective_id=0, has_side_effects=True, vmem_limit_bytes=56 << 20
        ),
        name="factor",
    )(blocks, jnp.swapaxes(face_maps, 1, 2), *others)


def solution(mesh):
    return jax.shard_map(
        functools.partial(shards, (mesh.shape["gx"], mesh.shape["gy"])),
        mesh=mesh,
        in_specs=(
            P("gx", "gy", None, None, None),
            P(),
            P("gx", "gy", None, None, None),
            P("gx", "gy", None, None),
            P("gx", "gy", None),
            P("gx", "gy", None),
            P("gx", "gy", None, None),
            P("gx", "gy", None),
        ),
        out_specs=(P("gx", "gy", None, None, None), P("gx", "gy", None, None, None)),
        check_vma=False,
    )
```

```python
import functools

import jax
import jax.numpy as jnp
from jax import lax
from jax.experimental import pallas as pl
from jax.experimental.pallas import tpu as pltpu
from jax.sharding import PartitionSpec as P

MESH = pl.DeviceIdType.MESH
BF = jnp.bfloat16
F32 = jnp.float32
NN = (((1,), (0,)), ((), ()))
NT = (((1,), (1,)), ((), ()))
K = 64
M = 128
W = 32


def dot(left, right, dims):
    return lax.dot_general(left, right, dims, preferred_element_type=F32)


def split(x):
    high = x.astype(BF)
    low = (x - high.astype(F32)).astype(BF)
    return high, low


def lanes(*parts):
    return jnp.concatenate(parts, axis=1)


def rows(*parts):
    return jnp.concatenate(parts, axis=0)


def nn3(left, right):
    lh, ll = left
    rh, rl = right
    return dot(lanes(lh, ll, lh), rows(rh, rh, rl), NN)


def nt3(left, right):
    lh, ll = left
    rh, rl = right
    return dot(lanes(lh, ll, lh), lanes(rh, rh, rl), NT)


def iota(shape, dim):
    return lax.broadcasted_iota(jnp.int32, shape, dim)


def shifted(x, amount):
    amount = amount % M
    if amount == 0:
        return x
    return rows(x[M - amount :], x[: M - amount])


def invert(groups):
    n = len(groups)
    lane = iota((1, M), 1)
    scales = []
    for group in groups:
        top = jnp.maximum(*[jnp.max(x, axis=0, keepdims=True) for x in group])
        scale = jnp.ones((1, M), F32)
        for s in range(M // W):
            inside = lane // W == s
            scale = jnp.where(
                inside, jnp.max(jnp.where(inside, top, 0.0), axis=1, keepdims=True), scale
            )
        scales.append(1.0 / scale)
    tiles = [
        [jnp.stack([g[j][8 * i : 8 * i + 8] * sc for g, sc in zip(groups, scales)]) for j in range(2)]
        for i in range(8)
    ]
    sub = iota((n, 8, M), 1)
    within = iota((n, 8, M), 2) % W
    segment = iota((8 * n, 8, M), 2) // W * W
    for t in range(8):
        here, first = divmod(8 * t, W)
        source = jnp.concatenate([tiles[i][here] for i in range(8)], axis=0)
        cols = []
        for q in range(8):
            got = jnp.take_along_axis(source, segment + (first + q), axis=2, mode="promise_in_bounds")
            cols.append([got[n * i : n * i + n] for i in range(8)])
        unit = within == sub + first
        x = list(tiles[t])
        x[here] = jnp.where(
            (within >= first) & (within < first + 8), jnp.where(unit, 1.0, 0.0), x[here]
        )
        c = [cols[q][t] for q in range(8)]
        for k in range(8):
            inverse = 1.0 / c[k][:, k : k + 1, :]
            factor = jnp.where(sub == k, c[k] - 1.0, c[k])
            for q in range(k + 1, 8):
                c[q] = c[q] - factor * (c[q][:, k : k + 1, :] * inverse)
            x = [v - factor * (v[:, k : k + 1, :] * inverse) for v in x]
        r = list(x)
        r[here] = jnp.where(unit, x[here] + 1.0, x[here])
        for i in [(t + 1 + step) % 8 for step in range(7)]:
            for j in range(2):
                terms = [cols[q][i] * r[j][:, q : q + 1, :] for q in range(8)]
                while len(terms) > 1:
                    terms = [one + two for one, two in zip(terms[::2], terms[1::2])]
                tiles[i][j] = tiles[i][j] - terms[0]
        tiles[t] = x
    return [
        [jnp.concatenate([tiles[i][j][p] for i in range(8)], axis=0) * scales[p] for j in range(2)]
        for p in range(n)
    ]


def skeletonize(read_block, turn_of, counts, write, weigh=None, between=None):
    boxes = len(counts)
    row_of = iota((K, M), 0)
    lane_of = iota((K, M), 1)
    inner = lane_of % W
    segment = lane_of // W
    natural = [(lane_of + (M - W * r)) % M for r in range(4)]
    groups, sides, centres = [], [], []
    for g in range(0, boxes, 4):
        grams = []
        for r in range(4):
            ah, al = split(read_block(g + r))
            turn = turn_of(g + r)
            turned = split(dot(lanes(turn, turn), lanes(ah, al), NT))
            skel = tuple(shifted(x, -W * r)[:K] for x in turned)
            gram = nt3(skel, tuple(rows(x, shifted(x, -W)) for x in turned))
            if weigh is None:
                centres.append(dot(lanes(turn, turn), lanes(*turned), NT))
            live = (natural[r] >= counts[g + r]) & (row_of < counts[g + r])
            sides.append(split(jnp.where(live, gram[:, :M], 0.0)))
            grams.append(gram)
        count = jnp.where(
            segment < 2,
            jnp.where(segment == 0, counts[g], counts[g + 1]),
            jnp.where(segment == 2, counts[g + 2], counts[g + 3]),
        )
        group = []
        for j in range(2):
            parts = [x[:, M * j : M * j + M] for x in grams]
            normal = jnp.where(
                segment < 2,
                jnp.where(segment == 0, parts[0], parts[1]),
                jnp.where(segment == 2, parts[2], parts[3]),
            )
            column = inner + W * j
            normal = jnp.where((column < count) & (row_of < count), normal, 0.0)
            group.append(normal + jnp.where((column == row_of) & (row_of >= count), 1.0, 0.0))
        groups.append(group)
    inverses = invert(groups)
    shorts, parts = [], []
    chosen = iota((1, 2 * M), 1) % M // W
    for g in range(0, boxes, 4):
        inverse = split(lanes(*inverses[g // 4]))
        stacked = tuple(
            rows(*[x * jnp.where(chosen == r, 1.0, 0.0).astype(BF) for r in range(4)])
            for x in inverse
        )
        right = tuple(
            rows(*[sides[g + r][h][W * j : W * j + W] for j in range(2) for r in range(4)])
            for h in range(2)
        )
        interp = nn3(stacked, right)
        for r in range(4):
            keep = jnp.where((natural[r] == row_of) & (row_of < counts[g + r]), 1.0, 0.0)
            shorts.append(split(interp[K * r : K * r + K] + keep))
    if weigh is not None:
        for b in range(boxes):
            turn = turn_of(b)
            weights = dot(lanes(*shorts[b]), rows(turn, turn), NN)
            weigh(b, weights)
            parts.append(split(weights))
        between()
    for b in range(boxes):
        if weigh is None:
            left, middle = shorts[b], centres[b]
        else:
            left, middle = parts[b], read_block(b)
        applied = split(nn3(left, split(middle)))
        twice = tuple(rows(x, x) for x in left)
        pad = jnp.where((lane_of % K == row_of) & (row_of >= counts[b]), 1.0, 0.0)
        write(b, nt3(applied, twice) + pad)


def kernel(
    sizes,
    blocks_hbm, faces_hbm, couple_hbm, small_a, small_b, small_c, small_d, small_e,
    out_one, out_two,
    a_ref, face_ref, c_ref, turn_ref, own_ref, near_ref, send_c, near_c, mixed_ref,
    q_ref, child_w, child_z, send_w, send_z, level_w, level_z, cross_ref, parent_ref,
    order_one, order_two, count_one, count_two, merge_map,
    load_sems, send_sems, recv_sems,
):
    nx, ny = sizes
    gx, gy = lax.axis_index("gx"), lax.axis_index("gy")
    odd = gx % 2
    boxes = 8
    parents = 4

    loads = [pltpu.make_async_copy(blocks_hbm.at[0, 0, b], a_ref.at[b], load_sems.at[b]) for b in range(boxes)]
    load_face = pltpu.make_async_copy(faces_hbm, face_ref, load_sems.at[8])
    load_c = pltpu.make_async_copy(couple_hbm.at[0, 0], c_ref, load_sems.at[9])
    small_loads = [
        pltpu.make_async_copy(source, target, load_sems.at[10 + i])
        for i, (source, target) in enumerate(
            zip(
                (small_a, small_b, small_c, small_d, small_e),
                (order_one, count_one, merge_map, order_two, count_two),
            )
        )
    ]
    for load in small_loads + loads:
        load.start()
    load_face.start()
    load_c.start()

    barrier = pltpu.get_barrier_semaphore()
    sides = (
        (gx > 0, {"gx": gx - 1, "gy": gy}, 1),
        (gx < nx - 1, {"gx": gx + 1, "gy": gy}, 0),
        (gy > 0, {"gx": gx, "gy": gy - 1}, 3),
        (gy < ny - 1, {"gx": gx, "gy": gy + 1}, 2),
    )
    partner = {"gx": gx + 1 - 2 * odd, "gy": gy}
    for there, where, _ in sides:
        @pl.when(there)
        def _(where=where):
            pl.semaphore_signal(barrier, inc=1, device_id=where, device_id_type=MESH)

    for load in small_loads:
        load.wait()
    orders = rows(
        order_one[0, 0].astype(F32), order_two[0, 0].astype(F32), jnp.zeros((4, M), F32)
    ).T
    lane = iota((M, M), 1).astype(F32)

    def build_turn(b):
        turn_ref[b] = shifted(jnp.where(orders[:, b : b + 1] == lane, 1.0, 0.0).astype(BF), W * (b % 4))

    for b in range(boxes):
        build_turn(b)

    row_of = iota((K, M), 0)
    lane_of = iota((K, M), 1)
    left = lane_of < K
    counts = [count_one[0, 0, b] for b in range(boxes)]

    def copies(part):
        got = []
        for d, (there, where, face) in enumerate(sides):
            got.append((there, pltpu.make_async_remote_copy(
                src_ref=own_ref.at[part],
                dst_ref=near_ref.at[face, part],
                send_sem=send_sems.at[2 * d + part],
                recv_sem=recv_sems.at[2 * face + part],
                device_id=where,
                device_id_type=MESH,
            )))
        return got

    for part in range(2):
        for b in range(4 * part, 4 * part + 4, 2):
            halves = []
            for i in (0, 1):
                loads[b + i].wait()
                turn = shifted(turn_ref[b + i], -W * ((b + i) % 4))
                ah, al = split(a_ref[b + i])
                picked = split(dot(lanes(turn[:K], turn[:K]), rows(ah, al), NN))
                other = turn if i == 0 else rows(turn[K:], turn[:K])
                halves.append(dot(lanes(*picked), lanes(other, other), NT))
            c = jnp.where(left, counts[b], counts[b + 1])
            s = jnp.where(left, halves[0], halves[1])
            s = jnp.where((row_of < c) & (lane_of % K < c), s, 0.0)
            own_ref[part, (b % 4) // 2 * K : (b % 4) // 2 * K + K, :] = s
        if part == 0:
            pl.semaphore_wait(
                barrier,
                (gx + nx - 1) // nx + (2 * nx - 2 - gx) // nx
                + (gy + ny - 1) // ny + (2 * ny - 2 - gy) // ny,
            )
        for there, copy in reversed(copies(part)):
            @pl.when(there)
            def _(copy=copy):
                copy.start()

    m = [merge_map[0, 0, b] for b in range(boxes)]
    found = []
    for k in range(boxes):
        at = jnp.int32(0)
        for b in range(1, boxes):
            at = jnp.where(m[b] == k, b, at)
        found.append(at)
    is_odd = odd == 1
    send_box = [jnp.where(is_odd, found[k], k + 4) for k in range(parents)]
    keep_box = [jnp.where(is_odd, found[k + 4], k) for k in range(parents)]

    load_c.wait()
    for k in range(parents):
        send_c[k] = c_ref[send_box[k]]
    couple_copy = pltpu.make_async_remote_copy(
        src_ref=send_c, dst_ref=near_c, send_sem=send_sems.at[8], recv_sem=recv_sems.at[8],
        device_id=partner, device_id_type=MESH,
    )
    couple_copy.start()

    for k in range(parents):
        build_turn(boxes + k)

    for there, _, face in sides:
        @pl.when(jnp.logical_not(there))
        def _(face=face):
            near_ref[face ^ 1] = jnp.zeros((2, 2 * K, M), F32)

    load_face.wait()

    def mix_couples():
        couple_copy.wait_recv()
        for k in range(parents):
            mine, other = c_ref[keep_box[k]], near_c[k]
            first = jnp.where(is_odd, other, mine)
            second = jnp.where(is_odd, mine, other)
            mixed_ref[k] = first + second.T

    def project(f, source):
        face = split(face_ref[f])
        zero = jnp.zeros((K, M), BF)
        right = tuple(rows(lanes(x, zero), lanes(zero, x)) for x in face)
        return nn3(split(source), right)

    all_faces = split(face_ref[...].reshape(6 * K, M).T)
    for f in (4, 5):
        q = project(f, own_ref[...].reshape(4 * K, M))
        for b in range(boxes):
            p, i = b // 2, b % 2
            n = b + 1 if f == 4 else b - 1
            if 0 <= n < boxes:
                q_ref[n // 2, f * K : f * K + K, M * (n % 2) : M * (n % 2) + M] = (
                    q[p * K : p * K + K, M * i : M * i + M]
                )
        edge = 0 if f == 4 else boxes - 1
        q_ref[edge // 2, f * K : f * K + K, M * (edge % 2) : M * (edge % 2) + M] = jnp.zeros((K, M), F32)

    for f in range(4):
        if f == 2:
            mix_couples()
        there = sides[f][0]
        for part in range(2):
            @pl.when(there)
            def _(f=f, part=part):
                pltpu.make_async_remote_copy(
                    src_ref=own_ref.at[part],
                    dst_ref=near_ref.at[f, part],
                    send_sem=send_sems.at[2 * f + part],
                    recv_sem=recv_sems.at[2 * f + part],
                    device_id=sides[f][1],
                    device_id_type=MESH,
                ).wait_recv()
        q = project(f, near_ref[f].reshape(4 * K, M))
        for p in range(4):
            q_ref[p, f * K : f * K + K, :] = q[p * K : p * K + K]

    for p in range(4):
        d = nn3(all_faces, split(q_ref[p]))
        for i in (0, 1):
            a_ref[2 * p + i] = a_ref[2 * p + i] - d[:, M * i : M * i + M]

    def child_copy(i, source, target):
        return pltpu.make_async_remote_copy(
            src_ref=source, dst_ref=target.at[odd], send_sem=send_sems.at[9 + i],
            recv_sem=recv_sems.at[9 + i], device_id=partner, device_id_type=MESH,
        )

    w_copy = child_copy(0, send_w, child_w)
    z_copy = child_copy(1, send_z, child_z)

    def weigh(b, w):
        level_w[b] = w

    def send_weights():
        for k in range(parents):
            send_w[k] = level_w[send_box[k]]
        w_copy.start()
        for k in range(parents):
            child_w[odd, k] = level_w[keep_box[k]]

    def write_one(b, z):
        level_z[b] = z
        out_one[0, 0, b] = z[:, :K]

    skeletonize(
        lambda b: a_ref[b], lambda b: turn_ref[b], counts, write_one, weigh, send_weights
    )

    for k in range(parents):
        send_z[k] = level_z[send_box[k]]
    z_copy.start()
    for k in range(parents):
        child_z[odd, k] = level_z[keep_box[k]]

    w_copy.wait_recv()
    for k in range(parents):
        w_a = split(child_w[0, k])
        w_b = split(child_w[1, k])
        h = split(nn3(w_a, split(mixed_ref[k])))
        cross_ref[0, k] = nt3(h, tuple(rows(x, x) for x in w_b))
        cross_ref[1, k] = nt3(w_b, tuple(rows(x, x) for x in h))
    z_copy.wait_recv()
    for k in range(parents):
        parent_ref[k, :K] = jnp.where(left, child_z[0, k], cross_ref[0, k])
        parent_ref[k, K:] = jnp.where(left, cross_ref[1, k], child_z[1, k])

    def write_two(k, z):
        out_two[0, 0, k] = z[:, :K]

    skeletonize(
        lambda k: parent_ref[k], lambda k: turn_ref[boxes + k],
        [count_two[0, 0, k] for k in range(parents)], write_two,
    )

    for part in range(2):
        for there, copy in copies(part):
            @pl.when(there)
            def _(copy=copy):
                copy.wait_send()
    couple_copy.wait_send()
    w_copy.wait_send()
    z_copy.wait_send()


def shards(sizes, blocks, face_maps, *others):
    vmem = pl.BlockSpec(memory_space=pltpu.VMEM)
    hbm = pl.BlockSpec(memory_space=pltpu.HBM)
    return pl.pallas_call(
        functools.partial(kernel, sizes),
        out_shape=(
            jax.ShapeDtypeStruct((1, 1, 8, K, K), F32),
            jax.ShapeDtypeStruct((1, 1, 4, K, K), F32),
        ),
        in_specs=[hbm] * 8,
        out_specs=(vmem, vmem),
        scratch_shapes=[
            pltpu.VMEM((8, M, M), F32),
            pltpu.VMEM((6, K, M), F32),
            pltpu.VMEM((8, M, M), F32),
            pltpu.VMEM((12, M, M), BF),
            pltpu.VMEM((2, 2 * K, M), F32),
            pltpu.VMEM((4, 2, 2 * K, M), F32),
            pltpu.VMEM((4, M, M), F32),
            pltpu.VMEM((4, M, M), F32),
            pltpu.VMEM((4, M, M), F32),
            pltpu.VMEM((4, 6 * K, 2 * M), F32),
            pltpu.VMEM((2, 4, K, M), F32),
            pltpu.VMEM((2, 4, K, M), F32),
            pltpu.VMEM((4, K, M), F32),
            pltpu.VMEM((4, K, M), F32),
            pltpu.VMEM((8, K, M), F32),
            pltpu.VMEM((8, K, M), F32),
            pltpu.VMEM((2, 4, K, M), F32),
            pltpu.VMEM((4, M, M), F32),
            pltpu.VMEM((1, 1, 8, M), jnp.int32),
            pltpu.VMEM((1, 1, 4, M), jnp.int32),
            pltpu.SMEM((1, 1, 8), jnp.int32),
            pltpu.SMEM((1, 1, 4), jnp.int32),
            pltpu.SMEM((1, 1, 8), jnp.int32),
            pltpu.SemaphoreType.DMA((15,)),
            pltpu.SemaphoreType.DMA((11,)),
            pltpu.SemaphoreType.DMA((11,)),
        ],
        compiler_params=pltpu.CompilerParams(
            collective_id=0, has_side_effects=True, vmem_limit_bytes=56 << 20
        ),
        name="factor",
    )(blocks, jnp.swapaxes(face_maps, 1, 2), *others)


def solution(mesh):
    return jax.shard_map(
        functools.partial(shards, (mesh.shape["gx"], mesh.shape["gy"])),
        mesh=mesh,
        in_specs=(
            P("gx", "gy", None, None, None),
            P(),
            P("gx", "gy", None, None, None),
            P("gx", "gy", None, None),
            P("gx", "gy", None),
            P("gx", "gy", None),
            P("gx", "gy", None, None),
            P("gx", "gy", None),
        ),
        out_specs=(P("gx", "gy", None, None, None), P("gx", "gy", None, None, None)),
        check_vma=False,
    )
```

```python
import functools

import jax
import jax.numpy as jnp
from jax import lax
from jax.experimental import pallas as pl
from jax.experimental.pallas import tpu as pltpu
from jax.sharding import PartitionSpec as P

MESH = pl.DeviceIdType.MESH
BF = jnp.bfloat16
F32 = jnp.float32
NN = (((1,), (0,)), ((), ()))
NT = (((1,), (1,)), ((), ()))
K = 64
M = 128
W = 32


def dot(left, right, dims):
    return lax.dot_general(left, right, dims, preferred_element_type=F32)


def split(x):
    high = x.astype(BF)
    low = (x - high.astype(F32)).astype(BF)
    return high, low


def lanes(*parts):
    return jnp.concatenate(parts, axis=1)


def rows(*parts):
    return jnp.concatenate(parts, axis=0)


def nn3(left, right):
    lh, ll = left
    rh, rl = right
    return dot(lanes(lh, ll, lh), rows(rh, rh, rl), NN)


def nt3(left, right):
    lh, ll = left
    rh, rl = right
    return dot(lanes(lh, ll, lh), lanes(rh, rh, rl), NT)


def iota(shape, dim):
    return lax.broadcasted_iota(jnp.int32, shape, dim)


def shifted(x, amount):
    amount = amount % M
    if amount == 0:
        return x
    return rows(x[M - amount :], x[: M - amount])


def invert(groups):
    n = len(groups)
    lane = iota((1, M), 1)
    scales = []
    for group in groups:
        top = jnp.maximum(*[jnp.max(x, axis=0, keepdims=True) for x in group])
        scale = jnp.ones((1, M), F32)
        for s in range(M // W):
            inside = lane // W == s
            scale = jnp.where(
                inside, jnp.max(jnp.where(inside, top, 0.0), axis=1, keepdims=True), scale
            )
        scales.append(1.0 / scale)
    tiles = [
        [jnp.stack([g[j][8 * i : 8 * i + 8] * sc for g, sc in zip(groups, scales)]) for j in range(2)]
        for i in range(8)
    ]
    sub = iota((n, 8, M), 1)
    within = iota((n, 8, M), 2) % W
    segment = iota((1, 8, M), 2) // W * W

    def spread(parts, lane_at):
        source = jnp.concatenate(parts, axis=0)
        place = jnp.broadcast_to(segment + lane_at, source.shape)
        got = jnp.take_along_axis(source, place, axis=2, mode="promise_in_bounds")
        return [got[n * i : n * i + n] for i in range(len(parts))]

    def update(value, factors, row):
        terms = [f * row[:, q : q + 1, :] for q, f in enumerate(factors)]
        while len(terms) > 1:
            terms = [one + two for one, two in zip(terms[::2], terms[1::2])]
        return value - terms[0]

    c = [spread([tiles[0][0], tiles[1][0]], q)[0] for q in range(8)]
    for t in range(8):
        here, first = divmod(8 * t, W)
        after, start = divmod(8 * t + 8, W)
        ahead = [
            spread([tiles[t][after], tiles[t + 1][after]], start + q) for q in range(8)
        ] if t < 7 else []
        others = [(t + 1 + step) % 8 for step in range(7)]
        cols = [spread([tiles[i][here] for i in others], first + q) for q in range(8)]
        unit = within == sub + first
        x = list(tiles[t])
        x[here] = jnp.where(
            (within >= first) & (within < first + 8), jnp.where(unit, 1.0, 0.0), x[here]
        )
        same = [pair[0] for pair in ahead]
        for k in range(8):
            inverse = 1.0 / c[k][:, k : k + 1, :]
            factor = jnp.where(sub == k, c[k] - 1.0, c[k])
            for q in range(k + 1, 8):
                c[q] = c[q] - factor * (c[q][:, k : k + 1, :] * inverse)
            x = [v - factor * (v[:, k : k + 1, :] * inverse) for v in x]
            same = [v - factor * (v[:, k : k + 1, :] * inverse) for v in same]
        beside = [cols[q][0] for q in range(8)]
        c = [update(pair[1], beside, v) for pair, v in zip(ahead, same)]
        r = list(x)
        r[here] = jnp.where(unit, x[here] + 1.0, x[here])
        for m, i in enumerate(others):
            for j in range(2):
                tiles[i][j] = update(tiles[i][j], [cols[q][m] for q in range(8)], r[j])
        tiles[t] = x
    return [
        [jnp.concatenate([tiles[i][j][p] for i in range(8)], axis=0) * scales[p] for j in range(2)]
        for p in range(n)
    ]


def skeletonize(read_block, turn_of, counts, write, weigh=None, between=None):
    boxes = len(counts)
    row_of = iota((K, M), 0)
    lane_of = iota((K, M), 1)
    inner = lane_of % W
    segment = lane_of // W
    natural = [(lane_of + (M - W * r)) % M for r in range(4)]
    groups, sides, centres = [], [], []
    for g in range(0, boxes, 4):
        grams = []
        for r in range(4):
            ah, al = split(read_block(g + r))
            turn = turn_of(g + r)
            turned = split(dot(lanes(turn, turn), lanes(ah, al), NT))
            skel = tuple(shifted(x, -W * r)[:K] for x in turned)
            gram = nt3(skel, tuple(rows(x, shifted(x, -W)) for x in turned))
            if weigh is None:
                centres.append(dot(lanes(turn, turn), lanes(*turned), NT))
            live = (natural[r] >= counts[g + r]) & (row_of < counts[g + r])
            sides.append(split(jnp.where(live, gram[:, :M], 0.0)))
            grams.append(gram)
        count = jnp.where(
            segment < 2,
            jnp.where(segment == 0, counts[g], counts[g + 1]),
            jnp.where(segment == 2, counts[g + 2], counts[g + 3]),
        )
        group = []
        for j in range(2):
            parts = [x[:, M * j : M * j + M] for x in grams]
            normal = jnp.where(
                segment < 2,
                jnp.where(segment == 0, parts[0], parts[1]),
                jnp.where(segment == 2, parts[2], parts[3]),
            )
            column = inner + W * j
            normal = jnp.where((column < count) & (row_of < count), normal, 0.0)
            group.append(normal + jnp.where((column == row_of) & (row_of >= count), 1.0, 0.0))
        groups.append(group)
    inverses = invert(groups)
    shorts, parts = [], []
    chosen = iota((1, 2 * M), 1) % M // W
    for g in range(0, boxes, 4):
        inverse = split(lanes(*inverses[g // 4]))
        stacked = tuple(
            rows(*[x * jnp.where(chosen == r, 1.0, 0.0).astype(BF) for r in range(4)])
            for x in inverse
        )
        right = tuple(
            rows(*[sides[g + r][h][W * j : W * j + W] for j in range(2) for r in range(4)])
            for h in range(2)
        )
        interp = nn3(stacked, right)
        for r in range(4):
            keep = jnp.where((natural[r] == row_of) & (row_of < counts[g + r]), 1.0, 0.0)
            shorts.append(split(interp[K * r : K * r + K] + keep))
    if weigh is not None:
        for b in range(boxes):
            turn = turn_of(b)
            weights = dot(lanes(*shorts[b]), rows(turn, turn), NN)
            weigh(b, weights)
            parts.append(split(weights))
        between()
    for b in range(boxes):
        if weigh is None:
            left, middle = shorts[b], centres[b]
        else:
            left, middle = parts[b], read_block(b)
        applied = split(nn3(left, split(middle)))
        twice = tuple(rows(x, x) for x in left)
        pad = jnp.where((lane_of % K == row_of) & (row_of >= counts[b]), 1.0, 0.0)
        write(b, nt3(applied, twice) + pad)


def kernel(
    sizes,
    blocks_hbm, faces_hbm, couple_hbm, small_a, small_b, small_c, small_d, small_e,
    out_one, out_two,
    a_ref, face_ref, c_ref, turn_ref, own_ref, near_ref, send_c, near_c, mixed_ref,
    q_ref, child_w, child_z, send_w, send_z, level_w, level_z, cross_ref, parent_ref,
    order_one, order_two, count_one, count_two, merge_map,
    load_sems, send_sems, recv_sems,
):
    nx, ny = sizes
    gx, gy = lax.axis_index("gx"), lax.axis_index("gy")
    odd = gx % 2
    boxes = 8
    parents = 4

    loads = [pltpu.make_async_copy(blocks_hbm.at[0, 0, b], a_ref.at[b], load_sems.at[b]) for b in range(boxes)]
    load_face = pltpu.make_async_copy(faces_hbm, face_ref, load_sems.at[8])
    load_c = pltpu.make_async_copy(couple_hbm.at[0, 0], c_ref, load_sems.at[9])
    small_loads = [
        pltpu.make_async_copy(source, target, load_sems.at[10 + i])
        for i, (source, target) in enumerate(
            zip(
                (small_a, small_b, small_c, small_d, small_e),
                (order_one, count_one, merge_map, order_two, count_two),
            )
        )
    ]
    for load in small_loads + loads:
        load.start()
    load_face.start()
    load_c.start()

    barrier = pltpu.get_barrier_semaphore()
    sides = (
        (gx > 0, {"gx": gx - 1, "gy": gy}, 1),
        (gx < nx - 1, {"gx": gx + 1, "gy": gy}, 0),
        (gy > 0, {"gx": gx, "gy": gy - 1}, 3),
        (gy < ny - 1, {"gx": gx, "gy": gy + 1}, 2),
    )
    partner = {"gx": gx + 1 - 2 * odd, "gy": gy}
    for there, where, _ in sides:
        @pl.when(there)
        def _(where=where):
            pl.semaphore_signal(barrier, inc=1, device_id=where, device_id_type=MESH)

    for load in small_loads:
        load.wait()
    orders = rows(
        order_one[0, 0].astype(F32), order_two[0, 0].astype(F32), jnp.zeros((4, M), F32)
    ).T
    lane = iota((M, M), 1).astype(F32)

    def build_turn(b):
        turn_ref[b] = shifted(jnp.where(orders[:, b : b + 1] == lane, 1.0, 0.0).astype(BF), W * (b % 4))

    for b in range(boxes):
        build_turn(b)

    row_of = iota((K, M), 0)
    lane_of = iota((K, M), 1)
    left = lane_of < K
    counts = [count_one[0, 0, b] for b in range(boxes)]

    def copies(part):
        got = []
        for d, (there, where, face) in enumerate(sides):
            got.append((there, pltpu.make_async_remote_copy(
                src_ref=own_ref.at[part],
                dst_ref=near_ref.at[face, part],
                send_sem=send_sems.at[4 * d + part],
                recv_sem=recv_sems.at[4 * face + part],
                device_id=where,
                device_id_type=MESH,
            )))
        return got

    for part in range(4):
        halves = []
        for i in (0, 1):
            b = 2 * part + i
            loads[b].wait()
            turn = shifted(turn_ref[b], -W * (b % 4))
            ah, al = split(a_ref[b])
            picked = split(dot(lanes(turn[:K], turn[:K]), rows(ah, al), NN))
            other = turn if i == 0 else rows(turn[K:], turn[:K])
            halves.append(dot(lanes(*picked), lanes(other, other), NT))
        c = jnp.where(left, counts[2 * part], counts[2 * part + 1])
        s = jnp.where(left, halves[0], halves[1])
        own_ref[part] = jnp.where((row_of < c) & (lane_of % K < c), s, 0.0)
        if part == 0:
            pl.semaphore_wait(
                barrier,
                (gx + nx - 1) // nx + (2 * nx - 2 - gx) // nx
                + (gy + ny - 1) // ny + (2 * ny - 2 - gy) // ny,
            )
        for there, copy in reversed(copies(part)):
            @pl.when(there)
            def _(copy=copy):
                copy.start()

    m = [merge_map[0, 0, b] for b in range(boxes)]
    found = []
    for k in range(boxes):
        at = jnp.int32(0)
        for b in range(1, boxes):
            at = jnp.where(m[b] == k, b, at)
        found.append(at)
    is_odd = odd == 1
    send_box = [jnp.where(is_odd, found[k], k + 4) for k in range(parents)]
    keep_box = [jnp.where(is_odd, found[k + 4], k) for k in range(parents)]

    load_c.wait()
    for k in range(parents):
        send_c[k] = c_ref[send_box[k]]
    couple_copy = pltpu.make_async_remote_copy(
        src_ref=send_c, dst_ref=near_c, send_sem=send_sems.at[16], recv_sem=recv_sems.at[16],
        device_id=partner, device_id_type=MESH,
    )
    couple_copy.start()

    for k in range(parents):
        build_turn(boxes + k)

    for there, _, face in sides:
        @pl.when(jnp.logical_not(there))
        def _(face=face):
            near_ref[face ^ 1] = jnp.zeros((4, K, M), F32)

    load_face.wait()

    def mix_couples():
        couple_copy.wait_recv()
        for k in range(parents):
            mine, other = c_ref[keep_box[k]], near_c[k]
            first = jnp.where(is_odd, other, mine)
            second = jnp.where(is_odd, mine, other)
            mixed_ref[k] = first + second.T

    def project(f, source):
        face = split(face_ref[f])
        zero = jnp.zeros((K, M), BF)
        right = tuple(rows(lanes(x, zero), lanes(zero, x)) for x in face)
        return nn3(split(source), right)

    all_faces = split(face_ref[...].reshape(6 * K, M).T)
    for f in (4, 5):
        q = project(f, own_ref[...].reshape(4 * K, M))
        for b in range(boxes):
            p, i = b // 2, b % 2
            n = b + 1 if f == 4 else b - 1
            if 0 <= n < boxes:
                q_ref[n // 2, f * K : f * K + K, M * (n % 2) : M * (n % 2) + M] = (
                    q[p * K : p * K + K, M * i : M * i + M]
                )
        edge = 0 if f == 4 else boxes - 1
        q_ref[edge // 2, f * K : f * K + K, M * (edge % 2) : M * (edge % 2) + M] = jnp.zeros((K, M), F32)

    for f in range(4):
        if f == 2:
            mix_couples()
        there = sides[f][0]
        for part in range(4):
            @pl.when(there)
            def _(f=f, part=part):
                pltpu.make_async_remote_copy(
                    src_ref=own_ref.at[part],
                    dst_ref=near_ref.at[f, part],
                    send_sem=send_sems.at[4 * f + part],
                    recv_sem=recv_sems.at[4 * f + part],
                    device_id=sides[f][1],
                    device_id_type=MESH,
                ).wait_recv()
        q = project(f, near_ref[f].reshape(4 * K, M))
        for p in range(4):
            q_ref[p, f * K : f * K + K, :] = q[p * K : p * K + K]

    for p in range(4):
        d = nn3(all_faces, split(q_ref[p]))
        for i in (0, 1):
            a_ref[2 * p + i] = a_ref[2 * p + i] - d[:, M * i : M * i + M]

    def child_copy(i, source, target):
        return pltpu.make_async_remote_copy(
            src_ref=source, dst_ref=target.at[odd], send_sem=send_sems.at[17 + i],
            recv_sem=recv_sems.at[17 + i], device_id=partner, device_id_type=MESH,
        )

    w_copy = child_copy(0, send_w, child_w)
    z_copy = child_copy(1, send_z, child_z)

    def weigh(b, w):
        level_w[b] = w

    def send_weights():
        for k in range(parents):
            send_w[k] = level_w[send_box[k]]
        w_copy.start()
        for k in range(parents):
            child_w[odd, k] = level_w[keep_box[k]]

    def write_one(b, z):
        level_z[b] = z
        out_one[0, 0, b] = z[:, :K]

    skeletonize(
        lambda b: a_ref[b], lambda b: turn_ref[b], counts, write_one, weigh, send_weights
    )

    for k in range(parents):
        send_z[k] = level_z[send_box[k]]
    z_copy.start()
    for k in range(parents):
        child_z[odd, k] = level_z[keep_box[k]]

    w_copy.wait_recv()
    for k in range(parents):
        w_a = split(child_w[0, k])
        w_b = split(child_w[1, k])
        h = split(nn3(w_a, split(mixed_ref[k])))
        cross_ref[0, k] = nt3(h, tuple(rows(x, x) for x in w_b))
        cross_ref[1, k] = nt3(w_b, tuple(rows(x, x) for x in h))
    z_copy.wait_recv()
    for k in range(parents):
        parent_ref[k, :K] = jnp.where(left, child_z[0, k], cross_ref[0, k])
        parent_ref[k, K:] = jnp.where(left, cross_ref[1, k], child_z[1, k])

    def write_two(k, z):
        out_two[0, 0, k] = z[:, :K]

    skeletonize(
        lambda k: parent_ref[k], lambda k: turn_ref[boxes + k],
        [count_two[0, 0, k] for k in range(parents)], write_two,
    )

    for part in range(4):
        for there, copy in copies(part):
            @pl.when(there)
            def _(copy=copy):
                copy.wait_send()
    couple_copy.wait_send()
    w_copy.wait_send()
    z_copy.wait_send()


def shards(sizes, blocks, face_maps, *others):
    vmem = pl.BlockSpec(memory_space=pltpu.VMEM)
    hbm = pl.BlockSpec(memory_space=pltpu.HBM)
    results = pl.pallas_call(
        functools.partial(kernel, sizes),
        out_shape=(
            jax.ShapeDtypeStruct((1, 1, 8, K, K), F32),
            jax.ShapeDtypeStruct((1, 1, 4, K, K), F32),
        ),
        in_specs=[hbm] * 8,
        out_specs=(vmem, vmem),
        scratch_shapes=[
            pltpu.VMEM((8, M, M), F32),
            pltpu.VMEM((6, K, M), F32),
            pltpu.VMEM((8, M, M), F32),
            pltpu.VMEM((12, M, M), BF),
            pltpu.VMEM((4, K, M), F32),
            pltpu.VMEM((4, 4, K, M), F32),
            pltpu.VMEM((4, M, M), F32),
            pltpu.VMEM((4, M, M), F32),
            pltpu.VMEM((4, M, M), F32),
            pltpu.VMEM((4, 6 * K, 2 * M), F32),
            pltpu.VMEM((2, 4, K, M), F32),
            pltpu.VMEM((2, 4, K, M), F32),
            pltpu.VMEM((4, K, M), F32),
            pltpu.VMEM((4, K, M), F32),
            pltpu.VMEM((8, K, M), F32),
            pltpu.VMEM((8, K, M), F32),
            pltpu.VMEM((2, 4, K, M), F32),
            pltpu.VMEM((4, M, M), F32),
            pltpu.VMEM((1, 1, 8, M), jnp.int32),
            pltpu.VMEM((1, 1, 4, M), jnp.int32),
            pltpu.SMEM((1, 1, 8), jnp.int32),
            pltpu.SMEM((1, 1, 4), jnp.int32),
            pltpu.SMEM((1, 1, 8), jnp.int32),
            pltpu.SemaphoreType.DMA((15,)),
            pltpu.SemaphoreType.DMA((19,)),
            pltpu.SemaphoreType.DMA((19,)),
        ],
        compiler_params=pltpu.CompilerParams(
            collective_id=0, has_side_effects=True, vmem_limit_bytes=56 << 20
        ),
        name="factor",
    )(blocks, jnp.swapaxes(face_maps, 1, 2), *others)
    return pl.pallas_call(
        forward,
        out_shape=tuple(jax.ShapeDtypeStruct(x.shape, F32) for x in results),
        in_specs=[hbm] * 2,
        out_specs=(hbm, hbm),
        scratch_shapes=[pltpu.VMEM(x.shape, F32) for x in results]
        + [pltpu.SemaphoreType.DMA((4,))],
        compiler_params=pltpu.CompilerParams(vmem_limit_bytes=56 << 20),
        name="forward",
    )(*results)


def forward(one, two, out_one, out_two, held_one, held_two, sems):
    steps = ((one, held_one, out_one), (two, held_two, out_two))
    reads = [pltpu.make_async_copy(a, b, sems.at[i]) for i, (a, b, _) in enumerate(steps)]
    writes = [pltpu.make_async_copy(b, c, sems.at[2 + i]) for i, (_, b, c) in enumerate(steps)]
    for read in reads:
        read.start()
    for read, write in zip(reads, writes):
        read.wait()
        write.start()
    for write in writes:
        write.wait()


def solution(mesh):
    return jax.shard_map(
        functools.partial(shards, (mesh.shape["gx"], mesh.shape["gy"])),
        mesh=mesh,
        in_specs=(
            P("gx", "gy", None, None, None),
            P(),
            P("gx", "gy", None, None, None),
            P("gx", "gy", None, None),
            P("gx", "gy", None),
            P("gx", "gy", None),
            P("gx", "gy", None, None),
            P("gx", "gy", None),
        ),
        out_specs=(P("gx", "gy", None, None, None), P("gx", "gy", None, None, None)),
        check_vma=False,
    )
```

```python
import functools

import jax
import jax.numpy as jnp
from jax import lax
from jax.experimental import pallas as pl
from jax.experimental.pallas import tpu as pltpu
from jax.sharding import PartitionSpec as P

MESH = pl.DeviceIdType.MESH
BF = jnp.bfloat16
F32 = jnp.float32
NN = (((1,), (0,)), ((), ()))
NT = (((1,), (1,)), ((), ()))
K = 64
M = 128
W = 32


def dot(left, right, dims):
    return lax.dot_general(left, right, dims, preferred_element_type=F32)


def split(x):
    high = x.astype(BF)
    low = (x - high.astype(F32)).astype(BF)
    return high, low


def lanes(*parts):
    return jnp.concatenate(parts, axis=1)


def rows(*parts):
    return jnp.concatenate(parts, axis=0)


def nn3(left, right):
    lh, ll = left
    rh, rl = right
    return dot(lanes(lh, ll, lh), rows(rh, rh, rl), NN)


def nt3(left, right):
    lh, ll = left
    rh, rl = right
    return dot(lanes(lh, ll, lh), lanes(rh, rh, rl), NT)


def iota(shape, dim):
    return lax.broadcasted_iota(jnp.int32, shape, dim)


def shifted(x, amount):
    amount = amount % M
    if amount == 0:
        return x
    return rows(x[M - amount :], x[: M - amount])


def invert(groups):
    n = len(groups)
    lane = iota((1, M), 1)
    scales = []
    for group in groups:
        top = jnp.maximum(*[jnp.max(x, axis=0, keepdims=True) for x in group])
        scale = jnp.ones((1, M), F32)
        for s in range(M // W):
            inside = lane // W == s
            scale = jnp.where(
                inside, jnp.max(jnp.where(inside, top, 0.0), axis=1, keepdims=True), scale
            )
        scales.append(1.0 / scale)
    tiles = [
        [jnp.stack([g[j][8 * i : 8 * i + 8] * sc for g, sc in zip(groups, scales)]) for j in range(2)]
        for i in range(8)
    ]
    sub = iota((n, 8, M), 1)
    within = iota((n, 8, M), 2) % W
    segment = iota((1, 8, M), 2) // W * W

    def spread(parts, lane_at):
        source = jnp.concatenate(parts, axis=0)
        place = jnp.broadcast_to(segment + lane_at, source.shape)
        got = jnp.take_along_axis(source, place, axis=2, mode="promise_in_bounds")
        return [got[n * i : n * i + n] for i in range(len(parts))]

    def update(value, factors, row):
        terms = [f * row[:, q : q + 1, :] for q, f in enumerate(factors)]
        while len(terms) > 1:
            terms = [one + two for one, two in zip(terms[::2], terms[1::2])]
        return value - terms[0]

    c = [spread([tiles[0][0], tiles[1][0]], q)[0] for q in range(8)] if n == 1 else []
    for t in range(8):
        here, first = divmod(8 * t, W)
        after, start = divmod(8 * t + 8, W)
        ahead = [
            spread([tiles[t][after], tiles[t + 1][after]], start + q) for q in range(8)
        ] if t < 7 and n == 1 else []
        others = [(t + 1 + step) % 8 for step in range(7)]
        if n == 1:
            cols = [spread([tiles[i][here] for i in others], first + q) for q in range(8)]
        else:
            cols = [spread([tiles[t][here]] + [tiles[i][here] for i in others], first + q) for q in range(8)]
            c = [got[0] for got in cols]
            cols = [got[1:] for got in cols]
        unit = within == sub + first
        x = list(tiles[t])
        x[here] = jnp.where(
            (within >= first) & (within < first + 8), jnp.where(unit, 1.0, 0.0), x[here]
        )
        same = [pair[0] for pair in ahead]
        for k in range(8):
            inverse = 1.0 / c[k][:, k : k + 1, :]
            factor = jnp.where(sub == k, c[k] - 1.0, c[k])
            for q in range(k + 1, 8):
                c[q] = c[q] - factor * (c[q][:, k : k + 1, :] * inverse)
            x = [v - factor * (v[:, k : k + 1, :] * inverse) for v in x]
            same = [v - factor * (v[:, k : k + 1, :] * inverse) for v in same]
        beside = [cols[q][0] for q in range(8)]
        c = [update(pair[1], beside, v) for pair, v in zip(ahead, same)]
        r = list(x)
        r[here] = jnp.where(unit, x[here] + 1.0, x[here])
        for m, i in enumerate(others):
            for j in range(2):
                tiles[i][j] = update(tiles[i][j], [cols[q][m] for q in range(8)], r[j])
        tiles[t] = x
    return [
        [jnp.concatenate([tiles[i][j][p] for i in range(8)], axis=0) * scales[p] for j in range(2)]
        for p in range(n)
    ]


def skeletonize(read_block, turn_of, counts, write, weigh=None, between=None, ready=None):
    boxes = len(counts)
    row_of = iota((K, M), 0)
    lane_of = iota((K, M), 1)
    inner = lane_of % W
    segment = lane_of // W
    natural = [(lane_of + (M - W * r)) % M for r in range(4)]
    groups, sides, centres = [], [], []
    for g in range(0, boxes, 4):
        grams = []
        if ready is not None:
            ready(g)
        for r in range(4):
            ah, al = split(read_block(g + r))
            turn = turn_of(g + r)
            turned = split(dot(lanes(turn, turn), lanes(ah, al), NT))
            skel = tuple(shifted(x, -W * r)[:K] for x in turned)
            gram = nt3(skel, tuple(rows(x, shifted(x, -W)) for x in turned))
            if weigh is None:
                centres.append(dot(lanes(turn, turn), lanes(*turned), NT))
            live = (natural[r] >= counts[g + r]) & (row_of < counts[g + r])
            sides.append(split(jnp.where(live, gram[:, :M], 0.0)))
            grams.append(gram)
        count = jnp.where(
            segment < 2,
            jnp.where(segment == 0, counts[g], counts[g + 1]),
            jnp.where(segment == 2, counts[g + 2], counts[g + 3]),
        )
        group = []
        for j in range(2):
            parts = [x[:, M * j : M * j + M] for x in grams]
            normal = jnp.where(
                segment < 2,
                jnp.where(segment == 0, parts[0], parts[1]),
                jnp.where(segment == 2, parts[2], parts[3]),
            )
            column = inner + W * j
            normal = jnp.where((column < count) & (row_of < count), normal, 0.0)
            group.append(normal + jnp.where((column == row_of) & (row_of >= count), 1.0, 0.0))
        groups.append(group)
    inverses = invert(groups)
    shorts, parts = [], []
    chosen = iota((1, 2 * M), 1) % M // W
    for g in range(0, boxes, 4):
        inverse = split(lanes(*inverses[g // 4]))
        stacked = tuple(
            rows(*[x * jnp.where(chosen == r, 1.0, 0.0).astype(BF) for r in range(4)])
            for x in inverse
        )
        right = tuple(
            rows(*[sides[g + r][h][W * j : W * j + W] for j in range(2) for r in range(4)])
            for h in range(2)
        )
        interp = nn3(stacked, right)
        for r in range(4):
            keep = jnp.where((natural[r] == row_of) & (row_of < counts[g + r]), 1.0, 0.0)
            shorts.append(split(interp[K * r : K * r + K] + keep))
    if weigh is not None:
        for b in range(boxes):
            turn = turn_of(b)
            weights = dot(lanes(*shorts[b]), rows(turn, turn), NN)
            weigh(b, weights)
            parts.append(split(weights))
        between()
    for b in range(boxes):
        if weigh is None:
            left, middle = shorts[b], centres[b]
        else:
            left, middle = parts[b], read_block(b)
        applied = split(nn3(left, split(middle)))
        twice = tuple(rows(x, x) for x in left)
        pad = jnp.where((lane_of % K == row_of) & (row_of >= counts[b]), 1.0, 0.0)
        write(b, nt3(applied, twice) + pad)


def build_turns(order, turn_ref):
    boxes = order.shape[0]
    orders = rows(order.astype(F32), jnp.zeros((16 - boxes, M), F32)).T
    lane = iota((M, M), 1).astype(F32)
    for b in range(boxes):
        turn_ref[b] = shifted(
            jnp.where(orders[:, b : b + 1] == lane, 1.0, 0.0).astype(BF), W * (b % 4)
        )


def kernel(
    sizes,
    blocks_hbm, faces_hbm, couple_hbm, small_a, small_b, small_c,
    z_hbm, parents_hbm,
    a_ref, face_ref, c_ref, turn_ref, own_ref, near_ref, send_c, near_c, mixed_ref,
    q_ref, child_w, child_z, send_w, send_z, level_w, level_z, cross_ref, parent_ref,
    order_one, count_one, merge_map,
    load_sems, send_sems, recv_sems,
):
    nx, ny = sizes
    gx, gy = lax.axis_index("gx"), lax.axis_index("gy")
    odd = gx % 2
    boxes = 8
    parents = 4

    loads = [pltpu.make_async_copy(blocks_hbm.at[0, 0, b], a_ref.at[b], load_sems.at[b]) for b in range(boxes)]
    load_face = pltpu.make_async_copy(faces_hbm, face_ref, load_sems.at[8])
    load_c = pltpu.make_async_copy(couple_hbm.at[0, 0], c_ref, load_sems.at[9])
    small_loads = [
        pltpu.make_async_copy(source, target, load_sems.at[10 + i])
        for i, (source, target) in enumerate(
            zip(
                (small_a, small_b, small_c), (order_one, count_one, merge_map)
            )
        )
    ]
    for load in small_loads + loads:
        load.start()
    load_face.start()
    load_c.start()

    barrier = pltpu.get_barrier_semaphore()
    sides = (
        (gx > 0, {"gx": gx - 1, "gy": gy}, 1),
        (gx < nx - 1, {"gx": gx + 1, "gy": gy}, 0),
        (gy > 0, {"gx": gx, "gy": gy - 1}, 3),
        (gy < ny - 1, {"gx": gx, "gy": gy + 1}, 2),
    )
    partner = {"gx": gx + 1 - 2 * odd, "gy": gy}
    for there, where, _ in sides:
        @pl.when(there)
        def _(where=where):
            pl.semaphore_signal(barrier, inc=1, device_id=where, device_id_type=MESH)

    for load in small_loads:
        load.wait()
    build_turns(order_one[0, 0], turn_ref)

    row_of = iota((K, M), 0)
    lane_of = iota((K, M), 1)
    left = lane_of < K
    counts = [count_one[0, 0, b] for b in range(boxes)]

    def copies(part):
        got = []
        for d, (there, where, face) in enumerate(sides):
            got.append((there, pltpu.make_async_remote_copy(
                src_ref=own_ref.at[part],
                dst_ref=near_ref.at[face, part],
                send_sem=send_sems.at[4 * d + part],
                recv_sem=recv_sems.at[4 * face + part],
                device_id=where,
                device_id_type=MESH,
            )))
        return got

    for part in range(4):
        halves = []
        for i in (0, 1):
            b = 2 * part + i
            loads[b].wait()
            turn = shifted(turn_ref[b], -W * (b % 4))
            ah, al = split(a_ref[b])
            picked = split(dot(lanes(turn[:K], turn[:K]), rows(ah, al), NN))
            other = turn if i == 0 else rows(turn[K:], turn[:K])
            halves.append(dot(lanes(*picked), lanes(other, other), NT))
        c = jnp.where(left, counts[2 * part], counts[2 * part + 1])
        s = jnp.where(left, halves[0], halves[1])
        own_ref[part] = jnp.where((row_of < c) & (lane_of % K < c), s, 0.0)
        if part == 0:
            pl.semaphore_wait(
                barrier,
                (gx + nx - 1) // nx + (2 * nx - 2 - gx) // nx
                + (gy + ny - 1) // ny + (2 * ny - 2 - gy) // ny,
            )
        for there, copy in reversed(copies(part)):
            @pl.when(there)
            def _(copy=copy):
                copy.start()

    m = [merge_map[0, 0, b] for b in range(boxes)]
    found = []
    for k in range(boxes):
        at = jnp.int32(0)
        for b in range(1, boxes):
            at = jnp.where(m[b] == k, b, at)
        found.append(at)
    is_odd = odd == 1
    send_box = [jnp.where(is_odd, found[k], k + 4) for k in range(parents)]
    keep_box = [jnp.where(is_odd, found[k + 4], k) for k in range(parents)]

    load_c.wait()
    for k in range(parents):
        send_c[k] = c_ref[send_box[k]]
    couple_copy = pltpu.make_async_remote_copy(
        src_ref=send_c, dst_ref=near_c, send_sem=send_sems.at[16], recv_sem=recv_sems.at[16],
        device_id=partner, device_id_type=MESH,
    )
    couple_copy.start()

    for there, _, face in sides:
        @pl.when(jnp.logical_not(there))
        def _(face=face):
            near_ref[face ^ 1] = jnp.zeros((4, K, M), F32)

    load_face.wait()

    def mix_couples():
        couple_copy.wait_recv()
        for k in range(parents):
            mine, other = c_ref[keep_box[k]], near_c[k]
            first = jnp.where(is_odd, other, mine)
            second = jnp.where(is_odd, mine, other)
            mixed_ref[k] = first + second.T

    def project(f, source):
        face = split(face_ref[f])
        zero = jnp.zeros((K, M), BF)
        right = tuple(rows(lanes(x, zero), lanes(zero, x)) for x in face)
        return nn3(split(source), right)

    all_faces = split(face_ref[...].reshape(6 * K, M).T)
    for f in (4, 5):
        q = project(f, own_ref[...].reshape(4 * K, M))
        for b in range(boxes):
            p, i = b // 2, b % 2
            n = b + 1 if f == 4 else b - 1
            if 0 <= n < boxes:
                q_ref[n // 2, f * K : f * K + K, M * (n % 2) : M * (n % 2) + M] = (
                    q[p * K : p * K + K, M * i : M * i + M]
                )
        edge = 0 if f == 4 else boxes - 1
        q_ref[edge // 2, f * K : f * K + K, M * (edge % 2) : M * (edge % 2) + M] = jnp.zeros((K, M), F32)

    def receive(f, first, last):
        for part in range(first, last):
            @pl.when(sides[f][0])
            def _(part=part):
                pltpu.make_async_remote_copy(
                    src_ref=own_ref.at[part],
                    dst_ref=near_ref.at[f, part],
                    send_sem=send_sems.at[4 * f + part],
                    recv_sem=recv_sems.at[4 * f + part],
                    device_id=sides[f][1],
                    device_id_type=MESH,
                ).wait_recv()
        q = project(f, near_ref[f, first:last].reshape((last - first) * K, M))
        for p in range(first, last):
            q_ref[p, f * K : f * K + K, :] = q[(p - first) * K : (p - first) * K + K]

    receive(0, 0, 4)
    receive(1, 0, 4)
    mix_couples()

    def ready(g):
        first = g // 2
        receive(2, first, first + 2)
        receive(3, first, first + 2)
        for p in range(first, first + 2):
            d = nn3(all_faces, split(q_ref[p]))
            for i in (0, 1):
                a_ref[2 * p + i] = a_ref[2 * p + i] - d[:, M * i : M * i + M]

    def child_copy(i, source, target):
        return pltpu.make_async_remote_copy(
            src_ref=source, dst_ref=target.at[odd], send_sem=send_sems.at[17 + i],
            recv_sem=recv_sems.at[17 + i], device_id=partner, device_id_type=MESH,
        )

    w_copy = child_copy(0, send_w, child_w)
    z_copy = child_copy(1, send_z, child_z)

    def weigh(b, w):
        level_w[b] = w

    def send_weights():
        for k in range(parents):
            send_w[k] = level_w[send_box[k]]
        w_copy.start()
        for k in range(parents):
            child_w[odd, k] = level_w[keep_box[k]]

    def write_one(b, z):
        level_z[b] = z

    skeletonize(
        lambda b: a_ref[b], lambda b: turn_ref[b], counts, write_one, weigh, send_weights, ready
    )

    for k in range(parents):
        send_z[k] = level_z[send_box[k]]
    z_copy.start()
    stores = [pltpu.make_async_copy(level_z, z_hbm, load_sems.at[13])]
    stores[0].start()
    for k in range(parents):
        child_z[odd, k] = level_z[keep_box[k]]

    w_copy.wait_recv()
    for k in range(parents):
        w_a = split(child_w[0, k])
        w_b = split(child_w[1, k])
        h = split(nn3(w_a, split(mixed_ref[k])))
        cross_ref[0, k] = nt3(h, tuple(rows(x, x) for x in w_b))
        cross_ref[1, k] = nt3(w_b, tuple(rows(x, x) for x in h))
    z_copy.wait_recv()
    for k in range(parents):
        parent_ref[k, :K] = jnp.where(left, child_z[0, k], cross_ref[0, k])
        parent_ref[k, K:] = jnp.where(left, cross_ref[1, k], child_z[1, k])
        stores.append(
            pltpu.make_async_copy(parent_ref.at[k], parents_hbm.at[k], load_sems.at[14 + k])
        )
        stores[-1].start()

    for part in range(4):
        for there, copy in copies(part):
            @pl.when(there)
            def _(copy=copy):
                copy.wait_send()
    for store in stores:
        store.wait()
    couple_copy.wait_send()
    w_copy.wait_send()
    z_copy.wait_send()


def second_level(
    z_hbm, parents_hbm, order_hbm, count_hbm, one_hbm, out_two,
    z_ref, parent_ref, order, count, turn_ref, one_ref, sems,
):
    loads = [
        pltpu.make_async_copy(source, target, sems.at[i])
        for i, (source, target) in enumerate((
            (order_hbm, order), (count_hbm, count), (parents_hbm, parent_ref), (z_hbm, z_ref)
        ))
    ]
    for load in loads:
        load.start()
    loads[0].wait()
    loads[1].wait()
    build_turns(order[0, 0], turn_ref)
    loads[3].wait()
    for b in range(8):
        one_ref[0, 0, b] = z_ref[b][:, :K]
    store = pltpu.make_async_copy(one_ref, one_hbm, sems.at[4])
    store.start()
    loads[2].wait()

    def write(k, z):
        out_two[0, 0, k] = z[:, :K]

    skeletonize(
        lambda k: parent_ref[k], lambda k: turn_ref[k],
        [count[0, 0, k] for k in range(4)], write,
    )
    store.wait()


def shards(sizes, blocks, face_maps, couple, order_one, count_one, merge_map, order_two, count_two):
    vmem = pl.BlockSpec(memory_space=pltpu.VMEM)
    hbm = pl.BlockSpec(memory_space=pltpu.HBM)
    results = pl.pallas_call(
        functools.partial(kernel, sizes),
        out_shape=(
            jax.ShapeDtypeStruct((8, K, M), F32),
            jax.ShapeDtypeStruct((4, M, M), F32),
        ),
        in_specs=[hbm] * 6,
        out_specs=(hbm, hbm),
        scratch_shapes=[
            pltpu.VMEM((8, M, M), F32),
            pltpu.VMEM((6, K, M), F32),
            pltpu.VMEM((8, M, M), F32),
            pltpu.VMEM((8, M, M), BF),
            pltpu.VMEM((4, K, M), F32),
            pltpu.VMEM((4, 4, K, M), F32),
            pltpu.VMEM((4, M, M), F32),
            pltpu.VMEM((4, M, M), F32),
            pltpu.VMEM((4, M, M), F32),
            pltpu.VMEM((4, 6 * K, 2 * M), F32),
            pltpu.VMEM((2, 4, K, M), F32),
            pltpu.VMEM((2, 4, K, M), F32),
            pltpu.VMEM((4, K, M), F32),
            pltpu.VMEM((4, K, M), F32),
            pltpu.VMEM((8, K, M), F32),
            pltpu.VMEM((8, K, M), F32),
            pltpu.VMEM((2, 4, K, M), F32),
            pltpu.VMEM((4, M, M), F32),
            pltpu.VMEM((1, 1, 8, M), jnp.int32),
            pltpu.SMEM((1, 1, 8), jnp.int32),
            pltpu.SMEM((1, 1, 8), jnp.int32),
            pltpu.SemaphoreType.DMA((18,)),
            pltpu.SemaphoreType.DMA((19,)),
            pltpu.SemaphoreType.DMA((19,)),
        ],
        compiler_params=pltpu.CompilerParams(
            collective_id=0, has_side_effects=True, vmem_limit_bytes=56 << 20
        ),
        name="factor",
    )(blocks, jnp.swapaxes(face_maps, 1, 2), couple, order_one, count_one, merge_map)
    return pl.pallas_call(
        second_level,
        out_shape=(
            jax.ShapeDtypeStruct((1, 1, 8, K, K), F32),
            jax.ShapeDtypeStruct((1, 1, 4, K, K), F32),
        ),
        in_specs=[hbm] * 4,
        out_specs=(hbm, vmem),
        scratch_shapes=[
            pltpu.VMEM((8, K, M), F32),
            pltpu.VMEM((4, M, M), F32),
            pltpu.VMEM((1, 1, 4, M), jnp.int32),
            pltpu.SMEM((1, 1, 4), jnp.int32),
            pltpu.VMEM((4, M, M), BF),
            pltpu.VMEM((1, 1, 8, K, K), F32),
            pltpu.SemaphoreType.DMA((5,)),
        ],
        compiler_params=pltpu.CompilerParams(vmem_limit_bytes=56 << 20),
        name="second_level",
    )(*results, order_two, count_two)


def solution(mesh):
    return jax.shard_map(
        functools.partial(shards, (mesh.shape["gx"], mesh.shape["gy"])),
        mesh=mesh,
        in_specs=(
            P("gx", "gy", None, None, None),
            P(),
            P("gx", "gy", None, None, None),
            P("gx", "gy", None, None),
            P("gx", "gy", None),
            P("gx", "gy", None),
            P("gx", "gy", None, None),
            P("gx", "gy", None),
        ),
        out_specs=(P("gx", "gy", None, None, None), P("gx", "gy", None, None, None)),
        check_vma=False,
    )
```

```python
import functools

import jax
import jax.numpy as jnp
from jax import lax
from jax.experimental import pallas as pl
from jax.experimental.pallas import tpu as pltpu
from jax.sharding import PartitionSpec as P

MESH = pl.DeviceIdType.MESH
BF = jnp.bfloat16
F32 = jnp.float32
NN = (((1,), (0,)), ((), ()))
NT = (((1,), (1,)), ((), ()))
K = 64
M = 128
W = 32


def dot(left, right, dims):
    return lax.dot_general(left, right, dims, preferred_element_type=F32)


def split(x):
    high = x.astype(BF)
    low = (x - high.astype(F32)).astype(BF)
    return high, low


def lanes(*parts):
    return jnp.concatenate(parts, axis=1)


def rows(*parts):
    return jnp.concatenate(parts, axis=0)


def nn3(left, right):
    lh, ll = left
    rh, rl = right
    return dot(lanes(lh, ll, lh), rows(rh, rh, rl), NN)


def nt3(left, right):
    lh, ll = left
    rh, rl = right
    return dot(lanes(lh, ll, lh), lanes(rh, rh, rl), NT)


def iota(shape, dim):
    return lax.broadcasted_iota(jnp.int32, shape, dim)


def shifted(x, amount):
    amount = amount % M
    if amount == 0:
        return x
    return rows(x[M - amount :], x[: M - amount])


def invert(groups):
    n = len(groups)
    lane = iota((1, M), 1)
    scales = []
    for group in groups:
        top = jnp.maximum(*[jnp.max(x, axis=0, keepdims=True) for x in group])
        scale = jnp.ones((1, M), F32)
        for s in range(M // W):
            inside = lane // W == s
            scale = jnp.where(
                inside, jnp.max(jnp.where(inside, top, 0.0), axis=1, keepdims=True), scale
            )
        scales.append(1.0 / scale)
    tiles = [
        [jnp.stack([g[j][8 * i : 8 * i + 8] * sc for g, sc in zip(groups, scales)]) for j in range(2)]
        for i in range(8)
    ]
    sub = iota((n, 8, M), 1)
    within = iota((n, 8, M), 2) % W
    segment = iota((1, 8, M), 2) // W * W

    def spread(parts, lane_at):
        source = jnp.concatenate(parts, axis=0)
        place = jnp.broadcast_to(segment + lane_at, source.shape)
        got = jnp.take_along_axis(source, place, axis=2, mode="promise_in_bounds")
        return [got[n * i : n * i + n] for i in range(len(parts))]

    def update(value, factors, row):
        terms = [f * row[:, q : q + 1, :] for q, f in enumerate(factors)]
        while len(terms) > 1:
            terms = [one + two for one, two in zip(terms[::2], terms[1::2])]
        return value - terms[0]

    c = [spread([tiles[0][0], tiles[1][0]], q)[0] for q in range(8)] if n == 1 else []
    for t in range(8):
        here, first = divmod(8 * t, W)
        after, start = divmod(8 * t + 8, W)
        ahead = [
            spread([tiles[t][after], tiles[t + 1][after]], start + q) for q in range(8)
        ] if t < 7 and n == 1 else []
        others = [(t + 1 + step) % 8 for step in range(7)]
        if n == 1:
            cols = [spread([tiles[i][here] for i in others], first + q) for q in range(8)]
        else:
            cols = [spread([tiles[t][here]] + [tiles[i][here] for i in others], first + q) for q in range(8)]
            c = [got[0] for got in cols]
            cols = [got[1:] for got in cols]
        unit = within == sub + first
        x = list(tiles[t])
        x[here] = jnp.where(
            (within >= first) & (within < first + 8), jnp.where(unit, 1.0, 0.0), x[here]
        )
        same = [pair[0] for pair in ahead]
        for k in range(8):
            inverse = 1.0 / c[k][:, k : k + 1, :]
            factor = jnp.where(sub == k, c[k] - 1.0, c[k])
            for q in range(k + 1, 8):
                c[q] = c[q] - factor * (c[q][:, k : k + 1, :] * inverse)
            x = [v - factor * (v[:, k : k + 1, :] * inverse) for v in x]
            same = [v - factor * (v[:, k : k + 1, :] * inverse) for v in same]
        beside = [cols[q][0] for q in range(8)]
        c = [update(pair[1], beside, v) for pair, v in zip(ahead, same)]
        r = list(x)
        r[here] = jnp.where(unit, x[here] + 1.0, x[here])
        for m, i in enumerate(others):
            for j in range(2):
                tiles[i][j] = update(tiles[i][j], [cols[q][m] for q in range(8)], r[j])
        tiles[t] = x
    return [
        [jnp.concatenate([tiles[i][j][p] for i in range(8)], axis=0) * scales[p] for j in range(2)]
        for p in range(n)
    ]


def skeletonize(read_block, turn_of, counts, write, weigh=None, between=None):
    boxes = len(counts)
    row_of = iota((K, M), 0)
    lane_of = iota((K, M), 1)
    inner = lane_of % W
    segment = lane_of // W
    natural = [(lane_of + (M - W * r)) % M for r in range(4)]
    groups, sides, centres = [], [], []
    for g in range(0, boxes, 4):
        grams = []
        for r in range(4):
            ah, al = split(read_block(g + r))
            turn = turn_of(g + r)
            turned = split(dot(lanes(turn, turn), lanes(ah, al), NT))
            skel = tuple(shifted(x, -W * r)[:K] for x in turned)
            gram = nt3(skel, tuple(rows(x, shifted(x, -W)) for x in turned))
            if weigh is None:
                centres.append(dot(lanes(turn, turn), lanes(*turned), NT))
            live = (natural[r] >= counts[g + r]) & (row_of < counts[g + r])
            sides.append(split(jnp.where(live, gram[:, :M], 0.0)))
            grams.append(gram)
        count = jnp.where(
            segment < 2,
            jnp.where(segment == 0, counts[g], counts[g + 1]),
            jnp.where(segment == 2, counts[g + 2], counts[g + 3]),
        )
        group = []
        for j in range(2):
            parts = [x[:, M * j : M * j + M] for x in grams]
            normal = jnp.where(
                segment < 2,
                jnp.where(segment == 0, parts[0], parts[1]),
                jnp.where(segment == 2, parts[2], parts[3]),
            )
            column = inner + W * j
            normal = jnp.where((column < count) & (row_of < count), normal, 0.0)
            group.append(normal + jnp.where((column == row_of) & (row_of >= count), 1.0, 0.0))
        groups.append(group)
    inverses = invert(groups)
    shorts, parts = [], []
    chosen = iota((1, 2 * M), 1) % M // W
    for g in range(0, boxes, 4):
        inverse = split(lanes(*inverses[g // 4]))
        stacked = tuple(
            rows(*[x * jnp.where(chosen == r, 1.0, 0.0).astype(BF) for r in range(4)])
            for x in inverse
        )
        right = tuple(
            rows(*[sides[g + r][h][W * j : W * j + W] for j in range(2) for r in range(4)])
            for h in range(2)
        )
        interp = nn3(stacked, right)
        for r in range(4):
            keep = jnp.where((natural[r] == row_of) & (row_of < counts[g + r]), 1.0, 0.0)
            shorts.append(split(interp[K * r : K * r + K] + keep))
    if weigh is not None:
        for b in range(boxes):
            turn = turn_of(b)
            weights = dot(lanes(*shorts[b]), rows(turn, turn), NN)
            weigh(b, weights)
            parts.append(split(weights))
        between()
    for b in range(boxes):
        if weigh is None:
            left, middle = shorts[b], centres[b]
        else:
            left, middle = parts[b], read_block(b)
        applied = split(nn3(left, split(middle)))
        twice = tuple(rows(x, x) for x in left)
        pad = jnp.where((lane_of % K == row_of) & (row_of >= counts[b]), 1.0, 0.0)
        write(b, nt3(applied, twice) + pad)


def kernel(
    sizes,
    blocks_hbm, faces_hbm, couple_hbm, small_a, small_b, small_c, small_d, small_e,
    out_one, out_two,
    a_ref, face_ref, c_ref, turn_ref, own_ref, near_ref, send_c, near_c, mixed_ref,
    q_ref, child_w, child_z, send_w, send_z, level_w, level_z, cross_ref, parent_ref,
    order_one, order_two, count_one, count_two, merge_map,
    load_sems, send_sems, recv_sems,
):
    nx, ny = sizes
    gx, gy = lax.axis_index("gx"), lax.axis_index("gy")
    odd = gx % 2
    boxes = 8
    parents = 4

    loads = [pltpu.make_async_copy(blocks_hbm.at[0, 0, b], a_ref.at[b], load_sems.at[b]) for b in range(boxes)]
    load_face = pltpu.make_async_copy(faces_hbm, face_ref, load_sems.at[8])
    load_c = pltpu.make_async_copy(couple_hbm.at[0, 0], c_ref, load_sems.at[9])
    small_loads = [
        pltpu.make_async_copy(source, target, load_sems.at[10 + i])
        for i, (source, target) in enumerate(
            zip(
                (small_a, small_b, small_c, small_d, small_e),
                (order_one, count_one, merge_map, order_two, count_two),
            )
        )
    ]
    for load in small_loads + loads:
        load.start()
    load_face.start()
    load_c.start()

    barrier = pltpu.get_barrier_semaphore()
    sides = (
        (gx > 0, {"gx": gx - 1, "gy": gy}, 1),
        (gx < nx - 1, {"gx": gx + 1, "gy": gy}, 0),
        (gy > 0, {"gx": gx, "gy": gy - 1}, 3),
        (gy < ny - 1, {"gx": gx, "gy": gy + 1}, 2),
    )
    partner = {"gx": gx + 1 - 2 * odd, "gy": gy}
    for there, where, _ in sides:
        @pl.when(there)
        def _(where=where):
            pl.semaphore_signal(barrier, inc=1, device_id=where, device_id_type=MESH)

    for load in small_loads:
        load.wait()
    orders = rows(
        order_one[0, 0].astype(F32), order_two[0, 0].astype(F32), jnp.zeros((4, M), F32)
    ).T
    lane = iota((M, M), 1).astype(F32)

    def build_turn(b):
        turn_ref[b] = shifted(jnp.where(orders[:, b : b + 1] == lane, 1.0, 0.0).astype(BF), W * (b % 4))

    for b in range(boxes):
        build_turn(b)

    row_of = iota((K, M), 0)
    lane_of = iota((K, M), 1)
    left = lane_of < K
    counts = [count_one[0, 0, b] for b in range(boxes)]

    def copies(part):
        got = []
        for d, (there, where, face) in enumerate(sides):
            got.append((there, pltpu.make_async_remote_copy(
                src_ref=own_ref.at[part],
                dst_ref=near_ref.at[face, part],
                send_sem=send_sems.at[4 * d + part],
                recv_sem=recv_sems.at[4 * face + part],
                device_id=where,
                device_id_type=MESH,
            )))
        return got

    for part in range(4):
        halves = []
        for i in (0, 1):
            b = 2 * part + i
            loads[b].wait()
            turn = shifted(turn_ref[b], -W * (b % 4))
            ah, al = split(a_ref[b])
            picked = split(dot(lanes(turn[:K], turn[:K]), rows(ah, al), NN))
            other = turn if i == 0 else rows(turn[K:], turn[:K])
            halves.append(dot(lanes(*picked), lanes(other, other), NT))
        c = jnp.where(left, counts[2 * part], counts[2 * part + 1])
        s = jnp.where(left, halves[0], halves[1])
        own_ref[part] = jnp.where((row_of < c) & (lane_of % K < c), s, 0.0)
        if part == 0:
            pl.semaphore_wait(
                barrier,
                (gx + nx - 1) // nx + (2 * nx - 2 - gx) // nx
                + (gy + ny - 1) // ny + (2 * ny - 2 - gy) // ny,
            )
        for there, copy in reversed(copies(part)):
            @pl.when(there)
            def _(copy=copy):
                copy.start()

    m = [merge_map[0, 0, b] for b in range(boxes)]
    found = []
    for k in range(boxes):
        at = jnp.int32(0)
        for b in range(1, boxes):
            at = jnp.where(m[b] == k, b, at)
        found.append(at)
    is_odd = odd == 1
    send_box = [jnp.where(is_odd, found[k], k + 4) for k in range(parents)]
    keep_box = [jnp.where(is_odd, found[k + 4], k) for k in range(parents)]

    load_c.wait()
    for k in range(parents):
        send_c[k] = c_ref[send_box[k]]
    couple_copy = pltpu.make_async_remote_copy(
        src_ref=send_c, dst_ref=near_c, send_sem=send_sems.at[16], recv_sem=recv_sems.at[16],
        device_id=partner, device_id_type=MESH,
    )
    couple_copy.start()

    for k in range(parents):
        build_turn(boxes + k)

    for there, _, face in sides:
        @pl.when(jnp.logical_not(there))
        def _(face=face):
            near_ref[face ^ 1] = jnp.zeros((4, K, M), F32)

    load_face.wait()

    def mix_couples():
        couple_copy.wait_recv()
        for k in range(parents):
            mine, other = c_ref[keep_box[k]], near_c[k]
            first = jnp.where(is_odd, other, mine)
            second = jnp.where(is_odd, mine, other)
            mixed_ref[k] = first + second.T

    def project(f, source):
        face = split(face_ref[f])
        zero = jnp.zeros((K, M), BF)
        right = tuple(rows(lanes(x, zero), lanes(zero, x)) for x in face)
        return nn3(split(source), right)

    all_faces = split(face_ref[...].reshape(6 * K, M).T)
    for f in (4, 5):
        q = project(f, own_ref[...].reshape(4 * K, M))
        for b in range(boxes):
            p, i = b // 2, b % 2
            n = b + 1 if f == 4 else b - 1
            if 0 <= n < boxes:
                q_ref[n // 2, f * K : f * K + K, M * (n % 2) : M * (n % 2) + M] = (
                    q[p * K : p * K + K, M * i : M * i + M]
                )
        edge = 0 if f == 4 else boxes - 1
        q_ref[edge // 2, f * K : f * K + K, M * (edge % 2) : M * (edge % 2) + M] = jnp.zeros((K, M), F32)

    for f in range(4):
        if f == 2:
            mix_couples()
        there = sides[f][0]
        for part in range(4):
            @pl.when(there)
            def _(f=f, part=part):
                pltpu.make_async_remote_copy(
                    src_ref=own_ref.at[part],
                    dst_ref=near_ref.at[f, part],
                    send_sem=send_sems.at[4 * f + part],
                    recv_sem=recv_sems.at[4 * f + part],
                    device_id=sides[f][1],
                    device_id_type=MESH,
                ).wait_recv()
        q = project(f, near_ref[f].reshape(4 * K, M))
        for p in range(4):
            q_ref[p, f * K : f * K + K, :] = q[p * K : p * K + K]

    for p in range(4):
        d = nn3(all_faces, split(q_ref[p]))
        for i in (0, 1):
            a_ref[2 * p + i] = a_ref[2 * p + i] - d[:, M * i : M * i + M]

    def child_copy(i, source, target):
        return pltpu.make_async_remote_copy(
            src_ref=source, dst_ref=target.at[odd], send_sem=send_sems.at[17 + i],
            recv_sem=recv_sems.at[17 + i], device_id=partner, device_id_type=MESH,
        )

    w_copy = child_copy(0, send_w, child_w)
    z_copy = child_copy(1, send_z, child_z)

    def weigh(b, w):
        level_w[b] = w

    def send_weights():
        for k in range(parents):
            send_w[k] = level_w[send_box[k]]
        w_copy.start()
        for k in range(parents):
            child_w[odd, k] = level_w[keep_box[k]]

    def write_one(b, z):
        level_z[b] = z
        out_one[0, 0, b] = z[:, :K]

    skeletonize(
        lambda b: a_ref[b], lambda b: turn_ref[b], counts, write_one, weigh, send_weights
    )

    for k in range(parents):
        send_z[k] = level_z[send_box[k]]
    z_copy.start()
    for k in range(parents):
        child_z[odd, k] = level_z[keep_box[k]]

    w_copy.wait_recv()
    for k in range(parents):
        w_a = split(child_w[0, k])
        w_b = split(child_w[1, k])
        h = split(nn3(w_a, split(mixed_ref[k])))
        cross_ref[0, k] = nt3(h, tuple(rows(x, x) for x in w_b))
        cross_ref[1, k] = nt3(w_b, tuple(rows(x, x) for x in h))
    z_copy.wait_recv()
    for k in range(parents):
        parent_ref[k, :K] = jnp.where(left, child_z[0, k], cross_ref[0, k])
        parent_ref[k, K:] = jnp.where(left, cross_ref[1, k], child_z[1, k])

    def write_two(k, z):
        out_two[0, 0, k] = z[:, :K]

    skeletonize(
        lambda k: parent_ref[k], lambda k: turn_ref[boxes + k],
        [count_two[0, 0, k] for k in range(parents)], write_two,
    )

    for part in range(4):
        for there, copy in copies(part):
            @pl.when(there)
            def _(copy=copy):
                copy.wait_send()
    couple_copy.wait_send()
    w_copy.wait_send()
    z_copy.wait_send()


def shards(sizes, blocks, face_maps, *others):
    vmem = pl.BlockSpec(memory_space=pltpu.VMEM)
    hbm = pl.BlockSpec(memory_space=pltpu.HBM)
    results = pl.pallas_call(
        functools.partial(kernel, sizes),
        out_shape=(
            jax.ShapeDtypeStruct((1, 1, 8, K, K), F32),
            jax.ShapeDtypeStruct((1, 1, 4, K, K), F32),
        ),
        in_specs=[hbm] * 8,
        out_specs=(vmem, vmem),
        scratch_shapes=[
            pltpu.VMEM((8, M, M), F32),
            pltpu.VMEM((6, K, M), F32),
            pltpu.VMEM((8, M, M), F32),
            pltpu.VMEM((12, M, M), BF),
            pltpu.VMEM((4, K, M), F32),
            pltpu.VMEM((4, 4, K, M), F32),
            pltpu.VMEM((4, M, M), F32),
            pltpu.VMEM((4, M, M), F32),
            pltpu.VMEM((4, M, M), F32),
            pltpu.VMEM((4, 6 * K, 2 * M), F32),
            pltpu.VMEM((2, 4, K, M), F32),
            pltpu.VMEM((2, 4, K, M), F32),
            pltpu.VMEM((4, K, M), F32),
            pltpu.VMEM((4, K, M), F32),
            pltpu.VMEM((8, K, M), F32),
            pltpu.VMEM((8, K, M), F32),
            pltpu.VMEM((2, 4, K, M), F32),
            pltpu.VMEM((4, M, M), F32),
            pltpu.VMEM((1, 1, 8, M), jnp.int32),
            pltpu.VMEM((1, 1, 4, M), jnp.int32),
            pltpu.SMEM((1, 1, 8), jnp.int32),
            pltpu.SMEM((1, 1, 4), jnp.int32),
            pltpu.SMEM((1, 1, 8), jnp.int32),
            pltpu.SemaphoreType.DMA((15,)),
            pltpu.SemaphoreType.DMA((19,)),
            pltpu.SemaphoreType.DMA((19,)),
        ],
        compiler_params=pltpu.CompilerParams(
            collective_id=0, has_side_effects=True, vmem_limit_bytes=56 << 20
        ),
        name="factor",
    )(blocks, jnp.swapaxes(face_maps, 1, 2), *others)
    return pl.pallas_call(
        forward,
        out_shape=tuple(jax.ShapeDtypeStruct(x.shape, F32) for x in results),
        in_specs=[hbm] * 2,
        out_specs=(hbm, hbm),
        scratch_shapes=[pltpu.VMEM(x.shape, F32) for x in results]
        + [pltpu.SemaphoreType.DMA((4,))],
        compiler_params=pltpu.CompilerParams(vmem_limit_bytes=56 << 20),
        name="forward",
    )(*results)


def forward(one, two, out_one, out_two, held_one, held_two, sems):
    steps = ((one, held_one, out_one), (two, held_two, out_two))
    reads = [pltpu.make_async_copy(a, b, sems.at[i]) for i, (a, b, _) in enumerate(steps)]
    writes = [pltpu.make_async_copy(b, c, sems.at[2 + i]) for i, (_, b, c) in enumerate(steps)]
    for read in reads:
        read.start()
    for read, write in zip(reads, writes):
        read.wait()
        write.start()
    for write in writes:
        write.wait()


def solution(mesh):
    return jax.shard_map(
        functools.partial(shards, (mesh.shape["gx"], mesh.shape["gy"])),
        mesh=mesh,
        in_specs=(
            P("gx", "gy", None, None, None),
            P(),
            P("gx", "gy", None, None, None),
            P("gx", "gy", None, None),
            P("gx", "gy", None),
            P("gx", "gy", None),
            P("gx", "gy", None, None),
            P("gx", "gy", None),
        ),
        out_specs=(P("gx", "gy", None, None, None), P("gx", "gy", None, None, None)),
        check_vma=False,
    )
```
